128 devices in a mesh: dp: 2 (over core), tile: 64 (over y, z, x).
Axes of the slice: x: 4, y: 4, z: 4, core: 2. Of those that a mesh axis runs over, the one named last changes fastest.
Arguments:
- tile_latents: bfloat16 [6016, 4096], P(('dp', 'tile')), parts along dimension 0, may hold values from -6 to 6
- tile_owner: int32 [6016], P(('dp', 'tile')), parts along dimension 0, may hold values from -1 to 63, as said below
- tile_position: int32 [6016], P(('dp', 'tile')), parts along dimension 0, may hold values from -1 to 23, as said below
- neighbour_owner: int32 [3072, 8], P(('dp', 'tile')), parts along dimension 0, may hold values from -1 to 63, as said below
- neighbour_slot: int32 [3072, 8], P(('dp', 'tile')), parts along dimension 0, may hold values from -1 to 23, as said below
- w_embed: bfloat16 [64, 2048], replicated, may hold values from -0.75 to 0.75
- norm_gain: float32 [2048], replicated, may hold values from 0.1 to 1.9
- w_query: bfloat16 [2048, 1024], replicated
- w_key: bfloat16 [2048, 1024], replicated
- w_value: bfloat16 [2048, 1024], replicated, may hold values from -0.125 to 0.125
- w_out: bfloat16 [1024, 2048], replicated, may hold values from -0.1875 to 0.1875
Outputs:
- mixed: bfloat16 [196608, 2048], P(('dp', 'tile')), parts along dimension 0
The draws below stay inside these ranges and needn't reach their ends.
There are 2 independent parts, one for each index of `dp`. The reference program is written for one: setup_inputs(seed, part) draws one part's arguments, and reference() takes and returns one part's arrays. A program takes and returns all parts, laid end to end along the dimension named above; an argument that names none is the same for every part. Nothing has to cross between parts.
Inputs may be any that keep to these rules, and one draw needn't show every extreme that they name: `tile_owner`: -1 marks an empty slot and a loader's live slots come first. Every owner receives exactly one tile for each of its 24 positions, at most 1 from one loader, and that most is reached; some loader fills all 47 slots. Taken loader by loader and slot by slot, the m-th live slot goes to owner (m + r) mod 64 at position m // 64, for one r of the draw. `tile_position`: -1 exactly on empty slots. `neighbour_owner`: rows follow the packed tile order (owner by owner, position by position). Images of at most 13 tiles a row are laid row by row in that order, so a tile's left neighbour is the tile before it and its right neighbour the tile after it. A neighbour on another owner lies on the owner just before or just after; on the next owner it is among the first 14 tiles, on the previous among the last 14, and both ends are reached. -1 marks a neighbour outside the tile's image. `neighbour_slot`: -1 exactly where neighbour_owner is -1.
All inputs are finite; a program needn't handle non-finite values.
Results may differ from the reference program's by a relative error of at most 0.0078.
Values may be sent and summed in bfloat16 or wider, within the bound.
A program may use at most 192 MiB of HBM per device.

```python
import math
import jax
import jax.numpy as jnp
from jax import lax

D = 2048
HEADS = 8
HEAD = 128
LAT = 64
SIDE = 8
RADIUS = 6
TILES = 24
TILE_VALUES = 4096
WIDEST = 13
SLOTS = 47
ALL_TILES = 1536
ALL_SLOTS = 3008


DIRECTIONS = ((-1, -1), (-1, 0), (-1, 1), (0, -1), (0, 1), (1, -1), (1, 0), (1, 1))


def loader_plan(key):
    loaders = ALL_SLOTS // SLOTS
    subkeys = jax.random.split(key, 3)
    pair_count = loaders // 2
    spread = jax.random.randint(subkeys[0], (pair_count,), -(TILES - 1), TILES)
    spread = spread.at[0].set(TILES - 1)
    loaded_counts = jnp.stack([TILES + spread, TILES - spread], axis=1).reshape(loaders)
    loaded_counts = loaded_counts[jax.random.permutation(subkeys[1], loaders)]
    starts = jnp.cumsum(loaded_counts) - loaded_counts
    rotation = jax.random.randint(subkeys[2], (), 0, loaders)
    ordering = jnp.arange(SLOTS)
    loaded = starts[:, None] + ordering[None, :]
    filled = ordering[None, :] < loaded_counts[:, None]
    owners = jnp.where(filled, (loaded + rotation) % loaders, -1)
    positions = jnp.where(filled, loaded // loaders, -1)
    return (owners.reshape(-1).astype(jnp.int32), positions.reshape(-1).astype(jnp.int32))


def image_layout(key):
    subkeys = jax.random.split(key, 2)
    widths = jax.random.randint(subkeys[0], (ALL_TILES,), 2, WIDEST + 1).at[0].set(WIDEST)
    heights = jax.random.randint(subkeys[1], (ALL_TILES,), 1, 9).at[0].set((TILES + 2 * WIDEST + 1) // WIDEST + 1)
    image_sizes = widths * heights
    starts = jnp.cumsum(image_sizes) - image_sizes
    tile_ids = jnp.arange(ALL_TILES)
    image_ids = jnp.sum((starts[None, :] <= tile_ids[:, None]).astype(jnp.int32), axis=1) - 1
    image_start = starts[image_ids]
    image_width = widths[image_ids]
    extent = jnp.minimum(image_sizes[image_ids], ALL_TILES - image_start)
    in_image = tile_ids - image_start
    tile_row = in_image // image_width
    tile_col = in_image % image_width
    owner_list = []
    slot_list = []
    for step_row, step_col in DIRECTIONS:
        target_row = tile_row + step_row
        target_col = tile_col + step_col
        neighbour_spot = target_row * image_width + target_col
        inside = (target_col >= 0) & (target_col < image_width) & (target_row >= 0) & (neighbour_spot < extent)
        target = image_start + neighbour_spot
        owner_list.append(jnp.where(inside, target // TILES, -1))
        slot_list.append(jnp.where(inside, target % TILES, -1))
    return (jnp.stack(owner_list, axis=1).astype(jnp.int32), jnp.stack(slot_list, axis=1).astype(jnp.int32))


def shared_weights(key):
    return jax.random.normal(key, (D, HEADS * HEAD), jnp.float32) * D ** (-0.5)


def draw_tile_owner(key, part):
    owners, positions = loader_plan(key)
    return owners


def draw_tile_position(key, part):
    owners, positions = loader_plan(key)
    return positions


def draw_neighbour_owner(key, part):
    owners, slots_found = image_layout(key)
    return owners


def draw_neighbour_slot(key, part):
    owners, slots_found = image_layout(key)
    return slots_found


def draw_w_query(key, part):
    base_weights = shared_weights(key)
    return base_weights.astype(jnp.bfloat16)


def draw_w_key(key, part):
    key = jax.random.fold_in(key, 6)
    subkeys = jax.random.split(key, 1)
    fresh_part = jax.random.normal(subkeys[0], (D, HEADS * HEAD), jnp.float32) * D ** (-0.5)
    return fresh_part.astype(jnp.bfloat16)


def steps_of(own_key, shape, shards, smallest, high):
    gain, own = 1.0, jax.random.fold_in(own_key, 6)
    for position, blocks in shards:
        steps = jnp.exp(jax.random.uniform(jax.random.fold_in(own, position), (blocks,), jnp.float32, smallest / len(shards), high / len(shards)))
        gain = gain * jnp.repeat(steps, shape[position] // blocks).reshape([-1 if axis == position else 1 for axis in range(len(shape))])
    return gain


def normal_values(key, dims, width, most, shards=(), held_as=jnp.bfloat16):
    array = width * jax.random.normal(key, dims, jnp.float32)
    if shards:
        array = array * steps_of(key, dims, shards, -0.22, 0.18)
    return jnp.clip(array, -most, most).astype(held_as)


def setup_inputs(seed: int = 0, part: int = 0) -> dict:
    key_list = jax.random.split(jax.random.key(seed), 12)
    own_keys = jax.random.split(jax.random.fold_in(key_list[11], part), 12)
    return {
        "tile_latents": normal_values(own_keys[0], (ALL_SLOTS, TILE_VALUES), 1.0, 6.0, ((0, 64),)),
        "tile_owner": draw_tile_owner(jax.random.fold_in(jax.random.fold_in(key_list[11], part), 71), part),
        "tile_position": draw_tile_position(jax.random.fold_in(jax.random.fold_in(key_list[11], part), 71), part),
        "neighbour_owner": draw_neighbour_owner(jax.random.fold_in(jax.random.fold_in(key_list[11], part), 71), part),
        "neighbour_slot": draw_neighbour_slot(jax.random.fold_in(jax.random.fold_in(key_list[11], part), 71), part),
        "w_embed": normal_values(key_list[5], (LAT, D), LAT ** -0.5, 0.75),
        "norm_gain": jnp.clip(1.0 + 0.18 * jax.random.normal(key_list[6], (D,), jnp.float32), 0.1, 1.9),
        "w_query": draw_w_query(jax.random.fold_in(key_list[11], 71), part),
        "w_key": draw_w_key(jax.random.fold_in(key_list[11], 71), part),
        "w_value": normal_values(key_list[9], (D, HEADS * HEAD), D ** -0.5, 0.125),
        "w_out": normal_values(key_list[10], (HEADS * HEAD, D), (HEADS * HEAD) ** -0.5, 0.1875),
    }


EPSILON = 1e-06

def window_mask():
    tile_tokens = SIDE * SIDE
    query_ids = jnp.arange(tile_tokens)
    key_ids = jnp.arange(9 * tile_tokens)
    region = key_ids // tile_tokens
    within = key_ids % tile_tokens
    offset_rows = (region // 3 - 1) * SIDE + within // SIDE
    offset_cols = (region % 3 - 1) * SIDE + within % SIDE
    offset_rows = offset_rows[None, :] - (query_ids // SIDE)[:, None]
    offset_cols = offset_cols[None, :] - (query_ids % SIDE)[:, None]
    return (jnp.abs(offset_rows) <= RADIUS) & (jnp.abs(offset_cols) <= RADIUS)

def normed_rows(latent_block, w_embed, norm_gain):
    token_rows = latent_block.reshape(-1, LAT)
    embedded = jnp.dot(token_rows, w_embed, preferred_element_type=jnp.float32)
    inverse_rms = lax.rsqrt(lax.optimization_barrier(jnp.mean(embedded * embedded, axis=-1, keepdims=True)) + EPSILON)
    return (embedded * inverse_rms * norm_gain).astype(jnp.bfloat16)

def attend_block(queries, gathered, present, mask_window, w_out):
    group_tiles = queries.shape[0]
    tile_tokens = queries.shape[1]
    key_heads = gathered[:, :, :, 0].reshape(group_tiles, 9 * tile_tokens, HEADS, HEAD).astype(jnp.float32)
    value_heads = gathered[:, :, :, 1].reshape(group_tiles, 9 * tile_tokens, HEADS, HEAD).astype(jnp.float32)
    query_heads = queries.reshape(group_tiles, tile_tokens, HEADS, HEAD).astype(jnp.float32)
    scores = jnp.einsum('gqhd,gkhd->ghqk', query_heads, key_heads) * HEAD ** (-0.5)
    allowed = mask_window[None, None] & jnp.repeat(present, tile_tokens, axis=1)[:, None, None, :]
    scores = jnp.where(allowed, scores, -jnp.inf)
    row_max = lax.optimization_barrier(jnp.max(scores, axis=-1, keepdims=True))
    raised = jnp.where(allowed, jnp.exp(scores - row_max), 0.0)
    totals = lax.optimization_barrier(jnp.sum(raised, axis=-1))
    weights = raised.astype(jnp.bfloat16)
    summed = jnp.einsum('ghqk,gkhd->gqhd', weights.astype(jnp.float32), value_heads)
    attended = (summed / jnp.transpose(totals, (0, 2, 1))[..., None]).astype(jnp.bfloat16)
    attended = attended.reshape(group_tiles * tile_tokens, HEADS * HEAD)
    return jnp.dot(attended, w_out, preferred_element_type=jnp.float32).astype(jnp.bfloat16)

def reference(tile_latents, tile_owner, tile_position, neighbour_owner, neighbour_slot, w_embed, norm_gain, w_query, w_key, w_value, w_out):
    tile_tokens = SIDE * SIDE
    head_width = HEADS * HEAD
    filled = tile_owner >= 0
    destination = jnp.where(filled, tile_owner * TILES + tile_position, ALL_TILES).astype(jnp.int32)
    owned_tiles = jnp.zeros((ALL_TILES, TILE_VALUES), jnp.bfloat16).at[destination].set(tile_latents, mode='drop')
    group_tiles = math.gcd(TILES, 8)
    step_count = ALL_TILES // group_tiles

    def project(latent_block):
        normed = normed_rows(latent_block, w_embed, norm_gain)
        query_part = jnp.dot(normed, w_query, preferred_element_type=jnp.float32).astype(jnp.bfloat16)
        key_part = jnp.dot(normed, w_key, preferred_element_type=jnp.float32).astype(jnp.bfloat16)
        value_part = jnp.dot(normed, w_value, preferred_element_type=jnp.float32).astype(jnp.bfloat16)
        shape_tiles = (group_tiles, tile_tokens, head_width)
        return (query_part.reshape(shape_tiles), jnp.stack([key_part.reshape(shape_tiles), value_part.reshape(shape_tiles)], axis=2))
    queries, key_values = lax.map(project, owned_tiles.reshape(step_count, group_tiles, TILE_VALUES))
    key_values = key_values.reshape(ALL_TILES, tile_tokens, 2, head_width)
    exists = neighbour_owner >= 0
    neighbour_index = jnp.where(exists, neighbour_owner * TILES + neighbour_slot, 0).astype(jnp.int32)
    self_index = jnp.arange(ALL_TILES, dtype=jnp.int32)[:, None]
    index_nine = jnp.concatenate([neighbour_index[:, :4], self_index, neighbour_index[:, 4:]], axis=1)
    present_nine = jnp.concatenate([exists[:, :4], jnp.ones((ALL_TILES, 1), dtype=bool), exists[:, 4:]], axis=1)
    mask_window = window_mask()

    def attend_step(inputs):
        query_block, index_block, present_block = inputs
        return attend_block(query_block, key_values[index_block], present_block, mask_window, w_out)
    result = lax.map(attend_step, (queries, index_nine.reshape(step_count, group_tiles, 9), present_nine.reshape(step_count, group_tiles, 9)))
    return result.reshape(ALL_TILES * tile_tokens, D)
```

```python
import math

import jax
import jax.numpy as jnp
import numpy as np
from jax import lax
from jax.experimental import pallas as pl
from jax.experimental.pallas import tpu as pltpu
from jax.sharding import PartitionSpec as P

D = 2048
HEADS = 8
HEAD = 128
LAT = 64
SIDE = 8
RADIUS = 6
HALO = 14
TILES = 24
EXT = TILES + 2 * HALO
EPSILON = 1e-06
AWAY = -1e38
GROUP = 4
SCALE = HEAD ** -0.5 * math.log2(math.e)

BF = jnp.bfloat16
F32 = jnp.float32


def place_constants():
    spread = np.zeros((GROUP, 2, 8, 8, GROUP, 8, 4), np.float32)
    for t in range(GROUP):
        for form in range(2):
            for r in range(8):
                for s in range(8):
                    spread[t, form, r, s, t, r, (s + 1 + 2 * form) % 4] = 1
    spread = spread.reshape(GROUP * 128, GROUP * 32)
    order = np.zeros((GROUP, 2, 2, 2, 4, 2, GROUP, 8, 4), np.float32)
    back = np.zeros((GROUP, 8, 8, GROUP, 2, 2, 2, 4, 2), np.float32)
    for t in range(GROUP):
        for a in range(2):
            for b in range(2):
                for p in range(2):
                    for r in range(4):
                        for c in range(2):
                            order[t, a, b, p, r, c, t, 4 * a + r, 2 * b + c] = 1
                            back[t, 4 * a + r, 4 * b + 2 * c + p, t, a, b, p, r, c] = 1
    order = order.reshape(GROUP * 64, GROUP * 32)
    back = back.reshape(GROUP * 64, GROUP * 64)
    query_extra = np.zeros((HEADS, 2, 4, 2, 128), np.float32)
    for p in range(2):
        for r in range(4):
            for c in range(2):
                query_extra[:, p, r, c, 8 + r] = 1
                query_extra[:, p, r, c, 12 + 2 * c + p] = 1
    query_extra = query_extra.reshape(HEADS * 16, 128)
    key_extra = np.zeros((2, 2, 2, 16, 8, 128), np.float32)
    for a in range(2):
        for b in range(2):
            for p in range(2):
                for row in range(16):
                    for s in range(8):
                        col = 2 * s + p
                        tile_row = (4 * a - 6 + row) // 8 + 1
                        tile_col = (4 * b - 6 + col) // 8 + 1
                        region = tile_row * 3 + tile_col
                        lane = key_extra[a, b, p, row, s]
                        if region != 4:
                            lane[region - (region > 4)] = 1
                        for i in range(4):
                            lane[8 + i] = 0 if i <= row <= i + 2 * RADIUS else AWAY
                            lane[12 + i] = 0 if i <= col <= i + 2 * RADIUS else AWAY
    key_extra = key_extra.reshape(4, 256, 128)
    as_bf = lambda x: np.asarray(x, np.float32).astype(jnp.bfloat16)
    return tuple(as_bf(x) for x in (spread, order, back, query_extra, key_extra))


def split(x):
    high = x.astype(BF)
    low = (x - high.astype(F32)).astype(BF)
    return high, low


def dot(a, b):
    return jnp.dot(a, b, preferred_element_type=F32)


def dot_t(a, b):
    return lax.dot_general(a, b, (((1,), (1,)), ((), ())), preferred_element_type=F32)


def attend_kernel(
    owner_ref, slot_ref, ext_ref, mix_ref, out_mix_ref, spread_ref, order_ref, back_ref,
    query_extra_ref, key_extra_ref, out_ref, z_ref, q_ref, u_ref,
):
    step = pl.program_id(0)
    me = lax.axis_index("tile")
    low_lane = lax.broadcasted_iota(jnp.int32, (16, 128), 1) < LAT

    @pl.when(step == 0)
    def _():
        rows = GROUP * 32
        spread = spread_ref[...]
        groups = EXT // GROUP
        for g in range(0, groups, 2):
            pair = [ext_ref[pl.ds(k * rows, rows), :] for k in range(g, min(g + 2, groups))]
            made = dot(spread, jnp.concatenate(pair, axis=1)).astype(BF)
            for k in range(len(pair)):
                z_ref[pl.ds((g + k) * GROUP * 128, GROUP * 128), :] = made[:, k * 128 : k * 128 + 128]
        order = order_ref[...]
        parity = (lax.broadcasted_iota(jnp.int32, (GROUP * 64, 128), 0) // 8) % 2
        half = lax.broadcasted_iota(jnp.int32, (GROUP * 64, 128), 1) // LAT
        keep = (parity == half).astype(F32)
        for g in range(TILES // GROUP):
            own = ext_ref[pl.ds(HALO * 32 + g * rows, rows), :]
            picked = (dot(order, own) * keep).astype(BF)
            both = jnp.concatenate([picked, picked], axis=1)
            q_ref[pl.ds(g * GROUP * 64, GROUP * 64), :] = dot(both, mix_ref[...]).astype(BF)

    sub = lax.broadcasted_iota(jnp.int32, (16, 128), 0) % 8
    lane_row = lax.broadcasted_iota(jnp.int32, (128, 128), 1)
    ones = jnp.ones((256, 128), BF)
    for t in range(GROUP):
        tile = step * GROUP + t
        places = []
        extra = query_extra_ref[...].astype(F32)
        for n in range(8):
            owner = owner_ref[tile, n]
            place = HALO + (owner - me) * TILES + slot_ref[tile, n]
            places.append(jnp.where(owner >= 0, place, HALO + tile))
            bias = jnp.where(owner >= 0, 0.0, AWAY).astype(F32)
            extra = jnp.where(lane_row == n, bias, extra)
        extra = extra.astype(BF)
        places = places[:4] + [HALO + tile] + places[4:]
        bases = [p * 128 for p in places]
        for b in range(2):
            strips = []
            for tile_row, pairs in ((0, (1, 2, 3)), (1, (0, 1, 2, 3)), (2, (0, 1, 2))):
                for pair in pairs:
                    left, mid, right = (
                        z_ref[pl.ds(pl.multiple_of(bases[tile_row * 3 + k] + b * 64 + pair * 16, 16), 16), :]
                        for k in range(3)
                    )
                    first, last = ((3, 7), (1, 5))[b]
                    strips.append(jnp.where(sub < first, left, jnp.where(sub < last, mid, right)))
            zero = jnp.zeros((16, 128), BF)
            even = [jnp.where(low_lane, s, zero) for s in strips]
            odd = [jnp.where(low_lane, zero, s) for s in strips]
            for a in range(2):
                quad = 2 * a + b
                cut = slice(2 * a, 2 * a + 8)
                held = jnp.concatenate(even[cut] + odd[cut], axis=0)
                keys = jnp.concatenate([held, key_extra_ref[quad]], axis=1)
                values = jnp.concatenate([held, ones], axis=1)
                block = q_ref[pl.ds(pl.multiple_of(tile * 64 + quad * 16, 16), 16), :]
                query = jnp.concatenate([block[:, h * 128 : h * 128 + 128] for h in range(HEADS)], axis=0)
                scores = dot_t(jnp.concatenate([query, extra], axis=1), keys)
                raised = jnp.exp2(scores - jnp.max(scores, axis=1, keepdims=True)).astype(BF)
                summed = dot(raised, values)
                part = summed[:, :128]
                part = (part + pltpu.roll(part, LAT, 1)) / summed[:, 128:]
                joined = [
                    jnp.where(low_lane, part[32 * k : 32 * k + 16], part[32 * k + 16 : 32 * k + 32])
                    for k in range(HEADS // 2)
                ]
                u_ref[pl.ds(t * 64 + quad * 16, 16), :] = jnp.concatenate(joined, axis=1).astype(BF)
    placed = dot(back_ref[...], u_ref[...]).astype(BF)
    for n in range(0, D, 512):
        out_ref[:, n : n + 512] = dot(placed, out_mix_ref[:, n : n + 512]).astype(BF)


def attend(owner, slot, ext, mix, out_mix):
    constants = place_constants()
    smem = pl.BlockSpec(memory_space=pltpu.SMEM)
    vmem = pl.BlockSpec(memory_space=pltpu.VMEM)
    rows = GROUP * 64
    return pl.pallas_call(
        attend_kernel,
        grid=(TILES // GROUP,),
        out_shape=jax.ShapeDtypeStruct((TILES * 64, D), BF),
        in_specs=[smem, smem] + [vmem] * 8,
        out_specs=pl.BlockSpec((rows, D), lambda i: (i, 0)),
        scratch_shapes=[
            pltpu.VMEM((EXT * 128, 128), BF),
            pltpu.VMEM((TILES * 64, HEADS * 128), BF),
            pltpu.VMEM((rows, HEADS * LAT), BF),
        ],
        compiler_params=pltpu.CompilerParams(vmem_limit_bytes=48 * 2**20),
        cost_estimate=pl.CostEstimate(flops=8 * 10**9, bytes_accessed=10**7, transcendentals=3 * 10**6),
        name="attend",
    )(owner, slot, ext, mix, out_mix, *[jnp.asarray(c) for c in constants])


CHUNK = 512


def fold_kernel(
    embed_ref, gain_ref, wq_ref, wk_ref, wv_ref, wo_ref, mix_ref, out_mix_ref,
    wq, wk, wv, wo, sems,
):
    copies = []
    for w, (source, target) in enumerate(((wq_ref, wq), (wk_ref, wk), (wv_ref, wv), (wo_ref, wo))):
        row_count = source.shape[0] // 4
        for c in range(4):
            cut = pl.ds(c * row_count, row_count)
            copy = pltpu.make_async_copy(source.at[cut], target.at[cut], sems.at[w, c])
            copy.start()
            copies.append(copy)
    scaled = embed_ref[...].astype(F32) * gain_ref[...]
    stacked = jnp.concatenate(split(scaled), axis=0)

    def folded(w, held):
        total = jnp.zeros((2 * LAT, HEADS * HEAD), F32)
        for c in range(4):
            copies[w * 4 + c].wait()
            total += dot(stacked[:, c * CHUNK : (c + 1) * CHUNK], held[pl.ds(c * CHUNK, CHUNK), :])
        return split(total[:LAT] + total[LAT:])

    query_high, query_low = folded(0, wq)
    key_high, key_low = folded(1, wk)
    for h in range(HEADS):
        cut = slice(h * HEAD, (h + 1) * HEAD)
        left = jnp.concatenate([query_high[:, cut], query_low[:, cut], query_high[:, cut]], axis=1)
        right = jnp.concatenate([key_high[:, cut], key_high[:, cut], key_low[:, cut]], axis=1)
        high, low = split(dot_t(left, jnp.concatenate([right, right], axis=0)) * SCALE)
        mix_ref[:, cut] = jnp.concatenate([high, high, low, low], axis=0)
    value = jnp.concatenate(folded(2, wv), axis=0)
    for h in range(HEADS):
        cut = slice(h * HEAD, (h + 1) * HEAD)
        if h % 2 == 0:
            copies[12 + h // 2].wait()
        for n in range(0, D, 512):
            made = dot(value[:, cut], wo[cut, n : n + 512])
            out_mix_ref[pl.ds(h * LAT, LAT), n : n + 512] = (made[:LAT] + made[LAT:]).astype(BF)


def fold(w_embed, norm_gain, w_query, w_key, w_value, w_out):
    vmem = pl.BlockSpec(memory_space=pltpu.VMEM)
    hbm = pl.BlockSpec(memory_space=pl.ANY)
    return pl.pallas_call(
        fold_kernel,
        out_shape=(
            jax.ShapeDtypeStruct((4 * LAT, HEADS * HEAD), BF),
            jax.ShapeDtypeStruct((HEADS * LAT, D), BF),
        ),
        in_specs=[vmem, vmem, hbm, hbm, hbm, hbm],
        out_specs=(vmem, vmem),
        scratch_shapes=[
            pltpu.VMEM(w.shape, BF) for w in (w_query, w_key, w_value, w_out)
        ] + [pltpu.SemaphoreType.DMA((4, 4))],
        compiler_params=pltpu.CompilerParams(vmem_limit_bytes=48 * 2**20),
        cost_estimate=pl.CostEstimate(flops=3 * 10**9, bytes_accessed=2 * 10**7, transcendentals=0),
        name="fold",
    )(w_embed, norm_gain.reshape(1, D), w_query, w_key, w_value, w_out)


def local(
    tile_latents, tile_owner, tile_position, neighbour_owner, neighbour_slot,
    w_embed, norm_gain, w_query, w_key, w_value, w_out,
):
    devices = lax.axis_size("tile")
    mix, out_mix = fold(w_embed, norm_gain, w_query, w_key, w_value, w_out)
    chosen = jnp.arange(devices)[:, None] == tile_owner[None, :]
    outgoing = dot(chosen.astype(BF), tile_latents)
    dead = ~jnp.any(chosen, axis=1, keepdims=True)
    outgoing = jnp.where(dead, 512.0, outgoing).astype(BF)
    arrived = lax.all_to_all(outgoing, "tile", split_axis=0, concat_axis=0, tiled=True)
    live = arrived[:, 0] < 100.0
    rank = jnp.cumsum(live.astype(jnp.int32)) - 1
    taken = (jnp.arange(TILES)[:, None] == rank[None, :]) & live[None, :]
    owned = dot(taken.astype(BF), arrived).reshape(TILES * 64, LAT)
    gram = dot_t(w_embed, w_embed) / D
    mean = jnp.sum(jnp.dot(owned, gram, precision=lax.Precision.HIGHEST) * owned, axis=1, keepdims=True)
    scaled = (owned * lax.rsqrt(jnp.maximum(mean, 0.0) + EPSILON)).astype(BF).reshape(TILES * 32, 128)
    up = [(i, (i + 1) % devices) for i in range(devices)]
    down = [(j, i) for i, j in up]
    before = lax.ppermute(scaled[(TILES - HALO) * 32 :], "tile", up)
    after = lax.ppermute(scaled[: HALO * 32], "tile", down)
    ext = jnp.concatenate([before, scaled, after], axis=0)
    return attend(neighbour_owner, neighbour_slot, ext, mix, out_mix)


def solution(mesh):
    both = P(("dp", "tile"), None)
    flat = P(("dp", "tile"))
    return jax.shard_map(
        local,
        mesh=mesh,
        in_specs=(both, flat, flat, both, both, P(), P(), P(), P(), P(), P()),
        out_specs=both,
        check_vma=False,
    )
```

```python
import math

import jax
import jax.numpy as jnp
import numpy as np
from jax import lax
from jax.experimental import pallas as pl
from jax.experimental.pallas import tpu as pltpu
from jax.sharding import PartitionSpec as P

D = 2048
HEADS = 8
HEAD = 128
LAT = 64
SIDE = 8
RADIUS = 6
HALO = 14
TILES = 24
TILE_VALUES = 4096
EXT = TILES + 2 * HALO
EPSILON = 1e-06
AWAY = -1e38
GROUP = 4
SCALE = HEAD ** -0.5 * math.log2(math.e)

BF = jnp.bfloat16
F32 = jnp.float32


def place_constants():
    spread = np.zeros((GROUP, 2, 8, 8, GROUP, 8, 4), np.float32)
    for t in range(GROUP):
        for form in range(2):
            for r in range(8):
                for s in range(8):
                    spread[t, form, r, s, t, r, (s + 1 + 2 * form) % 4] = 1
    spread = spread.reshape(GROUP * 128, GROUP * 32)
    order = np.zeros((GROUP, 2, 2, 2, 4, 2, GROUP, 8, 4), np.float32)
    back = np.zeros((GROUP, 8, 8, GROUP, 2, 2, 2, 4, 2), np.float32)
    for t in range(GROUP):
        for a in range(2):
            for b in range(2):
                for p in range(2):
                    for r in range(4):
                        for c in range(2):
                            order[t, a, b, p, r, c, t, 4 * a + r, 2 * b + c] = 1
                            back[t, 4 * a + r, 4 * b + 2 * c + p, t, a, b, p, r, c] = 1
    order = order.reshape(GROUP * 64, GROUP * 32)
    back = back.reshape(GROUP * 64, GROUP * 64)
    query_extra = np.zeros((HEADS, 2, 4, 2, 128), np.float32)
    for p in range(2):
        for r in range(4):
            for c in range(2):
                query_extra[:, p, r, c, 8 + r] = 1
                query_extra[:, p, r, c, 12 + 2 * c + p] = 1
    query_extra = query_extra.reshape(HEADS * 16, 128)
    key_extra = np.zeros((2, 2, 2, 16, 8, 128), np.float32)
    for a in range(2):
        for b in range(2):
            for p in range(2):
                for row in range(16):
                    for s in range(8):
                        col = 2 * s + p
                        tile_row = (4 * a - 6 + row) // 8 + 1
                        tile_col = (4 * b - 6 + col) // 8 + 1
                        region = tile_row * 3 + tile_col
                        lane = key_extra[a, b, p, row, s]
                        if region != 4:
                            lane[region - (region > 4)] = 1
                        for i in range(4):
                            lane[8 + i] = 0 if i <= row <= i + 2 * RADIUS else AWAY
                            lane[12 + i] = 0 if i <= col <= i + 2 * RADIUS else AWAY
    key_extra = key_extra.reshape(4, 256, 128)
    as_bf = lambda x: np.asarray(x, np.float32).astype(jnp.bfloat16)
    return tuple(as_bf(x) for x in (spread, order, back, query_extra, key_extra))


def split(x):
    high = x.astype(BF)
    low = (x - high.astype(F32)).astype(BF)
    return high, low


def dot(a, b):
    return jnp.dot(a, b, preferred_element_type=F32)


def dot_t(a, b):
    return lax.dot_general(a, b, (((1,), (1,)), ((), ())), preferred_element_type=F32)


LAG1, LAG2, LAG3 = 2, 4, 6


def attend_kernel(
    owner_ref, slot_ref, ext_ref, mix_ref, out_mix_ref, spread_ref, order_ref, back_ref,
    query_extra_ref, key_extra_ref, out_ref, z_ref, q_ref, u_ref,
):
    step = pl.program_id(0)
    me = lax.axis_index("tile")
    low_lane = lax.broadcasted_iota(jnp.int32, (16, 128), 1) < LAT

    @pl.when(step == 0)
    def _():
        rows = GROUP * 32
        spread = spread_ref[...]
        groups = EXT // GROUP
        for g in range(0, groups, 2):
            pair = [ext_ref[pl.ds(k * rows, rows), :] for k in range(g, min(g + 2, groups))]
            made = dot(spread, jnp.concatenate(pair, axis=1)).astype(BF)
            for k in range(len(pair)):
                z_ref[pl.ds((g + k) * GROUP * 128, GROUP * 128), :] = made[:, k * 128 : k * 128 + 128]
        order = order_ref[...]
        parity = (lax.broadcasted_iota(jnp.int32, (GROUP * 64, 128), 0) // 8) % 2
        half = lax.broadcasted_iota(jnp.int32, (GROUP * 64, 128), 1) // LAT
        keep = (parity == half).astype(F32)
        for g in range(TILES // GROUP):
            own = ext_ref[pl.ds(HALO * 32 + g * rows, rows), :]
            picked = (dot(order, own) * keep).astype(BF)
            both = jnp.concatenate([picked, picked], axis=1)
            q_ref[pl.ds(g * GROUP * 64, GROUP * 64), :] = dot(both, mix_ref[...]).astype(BF)

    sub = lax.broadcasted_iota(jnp.int32, (16, 128), 0) % 8
    lane_row = lax.broadcasted_iota(jnp.int32, (128, 128), 1)
    ones = jnp.ones((256, 128), BF)
    zero = jnp.zeros((16, 128), BF)

    def region(t):
        tile = step * GROUP + t
        places = []
        extra = query_extra_ref[...].astype(F32)
        for n in range(8):
            owner = owner_ref[tile, n]
            place = HALO + (owner - me) * TILES + slot_ref[tile, n]
            places.append(jnp.where(owner >= 0, place, HALO + tile))
            bias = jnp.where(owner >= 0, 0.0, AWAY).astype(F32)
            extra = jnp.where(lane_row == n, bias, extra)
        places = places[:4] + [HALO + tile] + places[4:]
        return tile, [p * 128 for p in places], extra.astype(BF)

    def window(bases, b):
        strips = []
        for tile_row, pairs in ((0, (1, 2, 3)), (1, (0, 1, 2, 3)), (2, (0, 1, 2))):
            for pair in pairs:
                left, mid, right = (
                    z_ref[pl.ds(pl.multiple_of(bases[tile_row * 3 + k] + b * 64 + pair * 16, 16), 16), :]
                    for k in range(3)
                )
                first, last = ((3, 7), (1, 5))[b]
                strips.append(jnp.where(sub < first, left, jnp.where(sub < last, mid, right)))
        return [jnp.where(low_lane, s, zero) for s in strips], [jnp.where(low_lane, zero, s) for s in strips]

    work = {}

    def start(i):
        t, b, a = i // 4, i // 2 % 2, i % 2
        quad = 2 * a + b
        if i % 4 == 0:
            work["region"] = region(t)
        tile, bases, extra = work["region"]
        if a == 0:
            work["window"] = window(bases, b)
        even, odd = work["window"]
        cut = slice(2 * a, 2 * a + 8)
        held = jnp.concatenate(even[cut] + odd[cut], axis=0)
        keys = jnp.concatenate([held, key_extra_ref[quad]], axis=1)
        block = q_ref[pl.ds(pl.multiple_of(tile * 64 + quad * 16, 16), 16), :]
        query = jnp.concatenate([block[:, h * 128 : h * 128 + 128] for h in range(HEADS)], axis=0)
        return held, dot_t(jnp.concatenate([query, extra], axis=1), keys)

    def soften(held, scores):
        raised = jnp.exp2(scores - jnp.max(scores, axis=1, keepdims=True)).astype(BF)
        return held, raised

    def gather(held, raised):
        return dot(raised, jnp.concatenate([held, ones], axis=1))

    def finish(i, summed):
        t, b, a = i // 4, i // 2 % 2, i % 2
        quad = 2 * a + b
        part = summed[:, :128]
        part = (part + pltpu.roll(part, LAT, 1)) / summed[:, 128:]
        joined = [
            jnp.where(low_lane, part[32 * k : 32 * k + 16], part[32 * k + 16 : 32 * k + 32])
            for k in range(HEADS // 2)
        ]
        u_ref[pl.ds(t * 64 + quad * 16, 16), :] = jnp.concatenate(joined, axis=1).astype(BF)

    count = GROUP * 4
    scored, softened, gathered = {}, {}, {}
    for i in range(count + LAG3):
        if i < count:
            scored[i] = start(i)
        j = i - LAG1
        if 0 <= j < count:
            softened[j] = soften(*scored.pop(j))
        j = i - LAG2
        if 0 <= j < count:
            gathered[j] = gather(*softened.pop(j))
        j = i - LAG3
        if 0 <= j < count:
            finish(j, gathered.pop(j))
    placed = dot(back_ref[...], u_ref[...]).astype(BF)
    for n in range(0, D, 512):
        out_ref[:, n : n + 512] = dot(placed, out_mix_ref[:, n : n + 512]).astype(BF)


def attend(owner, slot, ext, mix, out_mix):
    constants = place_constants()
    smem = pl.BlockSpec(memory_space=pltpu.SMEM)
    vmem = pl.BlockSpec(memory_space=pltpu.VMEM)
    rows = GROUP * 64
    return pl.pallas_call(
        attend_kernel,
        grid=(TILES // GROUP,),
        out_shape=jax.ShapeDtypeStruct((TILES * 64, D), BF),
        in_specs=[smem, smem] + [vmem] * 8,
        out_specs=pl.BlockSpec((rows, D), lambda i: (i, 0)),
        scratch_shapes=[
            pltpu.VMEM((EXT * 128, 128), BF),
            pltpu.VMEM((TILES * 64, HEADS * 128), BF),
            pltpu.VMEM((rows, HEADS * LAT), BF),
        ],
        compiler_params=pltpu.CompilerParams(vmem_limit_bytes=48 * 2**20),
        cost_estimate=pl.CostEstimate(flops=8 * 10**9, bytes_accessed=10**7, transcendentals=3 * 10**6),
        name="attend",
    )(owner, slot, ext, mix, out_mix, *[jnp.asarray(c) for c in constants])


CHUNK = 512
MESH = pl.DeviceIdType.MESH


def route_kernel(
    owner_ref, latents_ref, embed_ref, gain_ref, wq_ref, wk_ref, wv_ref, wo_ref,
    ext_ref, mix_ref, out_mix_ref,
    latents, wq, wk, wv, wo, stage, outbox, inbox, own, sems, local_sems,
    send_sem, recv_sem, halo_send, halo_recv,
):
    devices = lax.axis_size("tile")
    me = lax.axis_index("tile")
    edge = HALO * 32

    def load(index, source, target):
        copy = pltpu.make_async_copy(source, target, local_sems.at[index])
        copy.start()
        return copy

    loading = load(0, latents_ref, latents)
    copies = []
    for w, (source, target) in enumerate(((wq_ref, wq), (wk_ref, wk), (wv_ref, wv), (wo_ref, wo))):
        row_count = source.shape[0] // 4
        for c in range(4):
            cut = pl.ds(c * row_count, row_count)
            copy = pltpu.make_async_copy(source.at[cut], target.at[cut], sems.at[w, c])
            copy.start()
            copies.append(copy)

    barrier = pltpu.get_barrier_semaphore()

    def greet(k, carry):
        pl.semaphore_signal(barrier, inc=1, device_id={"tile": lax.rem(me + k, devices)}, device_id_type=MESH)
        return carry

    lax.fori_loop(1, devices, greet, 0)

    slots = owner_ref.shape[0]
    live = lax.fori_loop(0, slots, lambda j, n: n + jnp.where(owner_ref[j] >= 0, 1, 0), 0)
    dest = lax.broadcasted_iota(jnp.int32, (devices, slots), 0)
    slot = lax.broadcasted_iota(jnp.int32, (devices, slots), 1)
    first = owner_ref[0]
    chosen = jnp.where(((dest - first) % devices == slot) & (slot < live), 1.0, 0.0).astype(BF)
    row = lax.broadcasted_iota(jnp.int32, (devices, 128), 0)
    dead = jnp.where((row - first) % devices < live, 0.0, 512.0)
    loading.wait()
    for n in range(0, TILE_VALUES, 512):
        made = dot(chosen, latents[:, n : n + 512])
        for k in range(4):
            stage[pl.ds(n // 128 + k, devices, stride=32), :] = made[:, k * 128 : k * 128 + 128] + dead

    def pack(d, carry):
        outbox[d] = stage[pl.ds(pl.multiple_of(d * 32, 32), 32), :].astype(BF)
        return carry

    lax.fori_loop(0, devices, pack, 0)
    inbox[me] = outbox[me]
    pl.semaphore_wait(barrier, devices - 1)

    def send(k, carry):
        target = lax.rem(me + k, devices)
        pltpu.make_async_remote_copy(
            src_ref=outbox.at[target], dst_ref=inbox.at[me], send_sem=send_sem, recv_sem=recv_sem,
            device_id={"tile": target}, device_id_type=MESH,
        ).start()
        return carry

    lax.fori_loop(1, devices, send, 0)

    embed = embed_ref[...]
    scaled = embed.astype(F32) * gain_ref[...]
    stacked = jnp.concatenate(split(scaled), axis=0)
    twice = jnp.concatenate([embed, embed], axis=0)
    same = lax.broadcasted_iota(jnp.int32, (128, 128), 0) // LAT == lax.broadcasted_iota(jnp.int32, (128, 128), 1) // LAT
    gram = jnp.concatenate(split(jnp.where(same, dot_t(twice, twice) * (1.0 / D), 0.0)), axis=1)
    block = jnp.where(same, 1.0, 0.0).astype(BF)
    block = jnp.concatenate([block, block], axis=0)

    def folded(w, held):
        total = jnp.zeros((2 * LAT, HEADS * HEAD), F32)
        for c in range(4):
            copies[w * 4 + c].wait()
            total += dot(stacked[:, c * CHUNK : (c + 1) * CHUNK], held[pl.ds(c * CHUNK, CHUNK), :])
        return split(total[:LAT] + total[LAT:])

    query_high, query_low = folded(0, wq)
    key_high, key_low = folded(1, wk)
    for h in range(HEADS):
        cut = slice(h * HEAD, (h + 1) * HEAD)
        left = jnp.concatenate([query_high[:, cut], query_low[:, cut], query_high[:, cut]], axis=1)
        right = jnp.concatenate([key_high[:, cut], key_high[:, cut], key_low[:, cut]], axis=1)
        high, low = split(dot_t(left, jnp.concatenate([right, right], axis=0)) * SCALE)
        mix_ref[:, cut] = jnp.concatenate([high, high, low, low], axis=0)
    value = jnp.concatenate(folded(2, wv), axis=0)

    everyone = pltpu.make_async_remote_copy(
        src_ref=outbox.at[pl.ds(0, devices - 1)], dst_ref=inbox.at[pl.ds(0, devices - 1)],
        send_sem=send_sem, recv_sem=recv_sem, device_id={"tile": lax.rem(me + 1, devices)}, device_id_type=MESH,
    )
    everyone.wait_recv()

    lane = lax.broadcasted_iota(jnp.int32, (8, 128), 1)

    def rank(source, carry):
        seen, places = carry
        lives = inbox[source, 0:16, :].astype(F32)[:8] < 100.0
        seen = seen + jnp.where(lives, 1, 0)
        return seen, places + jnp.where(seen <= lane, 1, 0)

    zero = jnp.zeros((8, 128), jnp.int32)
    _, places = lax.fori_loop(0, devices, rank, (zero, zero))
    for p in range(TILES):
        own[pl.ds(p * 32, 32), :] = inbox[jnp.minimum(places[0, p], devices - 1)]
    held = own[...]
    tall = dot(held, gram)
    wide = held.astype(F32)
    mean = dot(jnp.concatenate(split((tall[:, :128] + tall[:, 128:]) * wide), axis=1), block)
    own[...] = (wide * lax.rsqrt(jnp.maximum(mean, 0.0) + EPSILON)).astype(BF)

    keep = load(1, own, ext_ref.at[pl.ds(edge, TILES * 32)])
    halos = []
    for side, (start, end, step) in enumerate((((TILES - HALO) * 32, 0, 1), (0, edge + TILES * 32, devices - 1))):
        copy = pltpu.make_async_remote_copy(
            src_ref=own.at[pl.ds(start, edge)], dst_ref=ext_ref.at[pl.ds(end, edge)],
            send_sem=halo_send.at[side], recv_sem=halo_recv.at[side],
            device_id={"tile": lax.rem(me + step, devices)}, device_id_type=MESH,
        )
        copy.start()
        halos.append(copy)

    for h in range(HEADS):
        cut = slice(h * HEAD, (h + 1) * HEAD)
        if h % 2 == 0:
            copies[12 + h // 2].wait()
        for n in range(0, D, 512):
            made = dot(value[:, cut], wo[cut, n : n + 512])
            out_mix_ref[pl.ds(h * LAT, LAT), n : n + 512] = (made[:LAT] + made[LAT:]).astype(BF)

    everyone.wait_send()
    for copy in halos:
        copy.wait()
    keep.wait()


def route(tile_owner, tile_latents, w_embed, norm_gain, w_query, w_key, w_value, w_out):
    devices = lax.axis_size("tile")
    vmem = pl.BlockSpec(memory_space=pltpu.VMEM)
    hbm = pl.BlockSpec(memory_space=pl.ANY)
    smem = pl.BlockSpec(memory_space=pltpu.SMEM)
    dma = pltpu.SemaphoreType.DMA
    return pl.pallas_call(
        route_kernel,
        out_shape=(
            jax.ShapeDtypeStruct((EXT * 32, 128), BF),
            jax.ShapeDtypeStruct((4 * LAT, HEADS * HEAD), BF),
            jax.ShapeDtypeStruct((HEADS * LAT, D), BF),
        ),
        in_specs=[smem, hbm, vmem, vmem, hbm, hbm, hbm, hbm],
        out_specs=(hbm, vmem, vmem),
        scratch_shapes=[pltpu.VMEM(tile_latents.shape, BF)]
        + [pltpu.VMEM(w.shape, BF) for w in (w_query, w_key, w_value, w_out)]
        + [
            pltpu.VMEM((devices * 32, 128), F32),
            pltpu.VMEM((devices, 32, 128), BF),
            pltpu.VMEM((devices, 32, 128), BF),
            pltpu.VMEM((TILES * 32, 128), BF),
            dma((4, 4)), dma((2,)), dma, dma, dma((2,)), dma((2,)),
        ],
        compiler_params=pltpu.CompilerParams(
            vmem_limit_bytes=48 * 2**20, collective_id=0, has_side_effects=True
        ),
        cost_estimate=pl.CostEstimate(flops=3 * 10**9, bytes_accessed=2 * 10**7, transcendentals=0),
        name="route",
    )(tile_owner, tile_latents, w_embed, norm_gain.reshape(1, D), w_query, w_key, w_value, w_out)


def local(
    tile_latents, tile_owner, tile_position, neighbour_owner, neighbour_slot,
    w_embed, norm_gain, w_query, w_key, w_value, w_out,
):
    ext, mix, out_mix = route(tile_owner, tile_latents, w_embed, norm_gain, w_query, w_key, w_value, w_out)
    return attend(neighbour_owner, neighbour_slot, ext, mix, out_mix)


def solution(mesh):
    both = P(("dp", "tile"), None)
    flat = P(("dp", "tile"))
    return jax.shard_map(
        local,
        mesh=mesh,
        in_specs=(both, flat, flat, both, both, P(), P(), P(), P(), P(), P()),
        out_specs=both,
        check_vma=False,
    )
```

```python
import math

import jax
import jax.numpy as jnp
import numpy as np
from jax import lax
from jax.experimental import pallas as pl
from jax.experimental.pallas import tpu as pltpu
from jax.sharding import PartitionSpec as P

D = 2048
HEADS = 8
HEAD = 128
LAT = 64
SIDE = 8
RADIUS = 6
HALO = 14
TILES = 24
TILE_VALUES = 4096
EXT = TILES + 2 * HALO
EPSILON = 1e-06
AWAY = -1e38
GROUP = 4
SCALE = 0.5 * HEAD ** -0.5 * math.log2(math.e)

BF = jnp.bfloat16
F32 = jnp.float32


def place_constants():
    double = np.zeros((2, LAT, 2, 2, LAT), np.float32)
    for p in range(2):
        for k in range(LAT):
            double[p, k, p, :, k] = 1
    double = double.reshape(128, 256)
    spread = np.zeros((GROUP, 2, 8, 8, GROUP, 8, 4), np.float32)
    for t in range(GROUP):
        for form in range(2):
            for r in range(8):
                for s in range(8):
                    spread[t, form, r, s, t, r, (s + 1 + 2 * form) % 4] = 1
    spread = spread.reshape(GROUP * 128, GROUP * 32)
    order = np.zeros((GROUP, 2, 2, 2, 4, 2, GROUP, 8, 4), np.float32)
    back = np.zeros((GROUP, 8, 8, GROUP, 2, 2, 2, 4, 2), np.float32)
    for t in range(GROUP):
        for a in range(2):
            for b in range(2):
                for p in range(2):
                    for r in range(4):
                        for c in range(2):
                            order[t, a, b, p, r, c, t, 4 * a + r, 2 * b + c] = 1
                            back[t, 4 * a + r, 4 * b + 2 * c + p, t, a, b, p, r, c] = 1
    order = order.reshape(GROUP * 64, GROUP * 32)
    back = back.reshape(GROUP * 64, GROUP * 64)
    query_extra = np.zeros((2, 4, 2, 128), np.float32)
    for p in range(2):
        for r in range(4):
            for c in range(2):
                query_extra[p, r, c, 8 + r] = 1
                query_extra[p, r, c, 12 + 2 * c + p] = 1
    query_extra = query_extra.reshape(16, 128)
    key_extra = np.zeros((2, 2, 2, 16, 8, 128), np.float32)
    for a in range(2):
        for b in range(2):
            for p in range(2):
                for row in range(16):
                    for s in range(8):
                        col = 2 * s + p
                        tile_row = (4 * a - 6 + row) // 8 + 1
                        tile_col = (4 * b - 6 + col) // 8 + 1
                        region = tile_row * 3 + tile_col
                        lane = key_extra[a, b, p, row, s]
                        if region != 4:
                            lane[region - (region > 4)] = 1
                        for i in range(4):
                            lane[8 + i] = 0 if i <= row <= i + 2 * RADIUS else AWAY
                            lane[12 + i] = 0 if i <= col <= i + 2 * RADIUS else AWAY
    key_extra = key_extra.reshape(1024, 128)
    stack = lambda x: np.concatenate([x[:, :128], x[:, 128:]], axis=0)
    moving = np.concatenate([stack(double), spread, order], axis=0).astype(jnp.bfloat16)
    fixed = np.concatenate([stack(back), query_extra, key_extra], axis=0).astype(jnp.bfloat16)
    return moving, fixed


def split(x):
    high = x.astype(BF)
    low = (x - high.astype(F32)).astype(BF)
    return high, low


def dot(a, b):
    return jnp.dot(a, b, preferred_element_type=F32)


def dot_t(a, b):
    return lax.dot_general(a, b, (((1,), (1,)), ((), ())), preferred_element_type=F32)


LAG1, LAG2, LAG3 = 2, 4, 6
OUT_AT = 3


def attend_kernel(
    owner_ref, slot_ref, z_ref, q_ref, out_mix_ref, fixed_ref, out_ref, u_ref, bias_ref, placed_ref, made_ref, sems,
):
    me = lax.axis_index("tile")
    low_lane = lax.broadcasted_iota(jnp.int32, (16, 128), 1) < LAT

    lane = lax.broadcasted_iota(jnp.int32, (16, 128), 1)
    sides = []
    for t in range(TILES):
        side = fixed_ref[pl.ds(512, 16), :].astype(F32)
        for n in range(8):
            side = jnp.where(lane == n, jnp.where(owner_ref[n, t] >= 0, 0.0, AWAY).astype(F32), side)
        sides.append(side.astype(BF))
    bias_ref[...] = dot_t(jnp.concatenate(sides, axis=0), fixed_ref[pl.ds(528, 1024), :])
    sub = lax.broadcasted_iota(jnp.int32, (16, 128), 0) % 8
    ones = jnp.ones((256, 128), BF)

    rows = GROUP * 64
    last = TILES // GROUP

    def place():
        placed_ref[...] = dot(jnp.concatenate([fixed_ref[0:256, :], fixed_ref[256:512, :]], axis=1), u_ref[...]).astype(BF)

    def copy_out(g):
        slot = g % 2
        return pltpu.make_async_copy(
            made_ref.at[slot], out_ref.at[pl.ds(pl.multiple_of(g * rows, rows), rows)], sems.at[slot]
        )

    def body(step, carry):
        @pl.when(step >= 3)
        def _():
            copy_out(step - 3).wait()

        place()
        slot = (step + 1) % 2

        def project(n):
            made_ref[slot, :, n * 512 : n * 512 + 512] = dot(
                placed_ref[...], out_mix_ref[:, n * 512 : n * 512 + 512]
            ).astype(BF)

        def region(t):
            tile = step * GROUP + t
            places = []
            for n in range(8):
                owner = owner_ref[n, tile]
                place = HALO + (owner - me) * TILES + slot_ref[n, tile]
                places.append(jnp.where(owner >= 0, place, HALO + tile))
            places = places[:4] + [HALO + tile] + places[4:]
            return tile, [p * 128 for p in places]

        def window(bases, b):
            first, last = ((3, 7), (1, 5))[b]
            sides = []
            for p in range(2):
                strips = []
                for tile_row, pairs in ((0, (1, 2, 3)), (1, (0, 1, 2, 3)), (2, (0, 1, 2))):
                    for pair in pairs:
                        left, mid, right = (
                            z_ref[p, pl.ds(pl.multiple_of(bases[tile_row * 3 + k] + b * 64 + pair * 16, 16), 16), :]
                            for k in range(3)
                        )
                        strips.append(jnp.where(sub < first, left, jnp.where(sub < last, mid, right)))
                sides.append(strips)
            return sides

        work = {}

        def start(i):
            t, b, a = i // 4, i // 2 % 2, i % 2
            quad = 2 * a + b
            if i % 4 == 0:
                work["region"] = region(t)
            tile, bases = work["region"]
            if a == 0:
                work["window"] = window(bases, b)
            even, odd = work["window"]
            cut = slice(2 * a, 2 * a + 8)
            held = jnp.concatenate(even[cut] + odd[cut], axis=0)
            block = q_ref[pl.ds(pl.multiple_of(tile * 64 + quad * 16, 16), 16), :]
            query = jnp.concatenate([block[:, h * 128 : h * 128 + 128] for h in range(HEADS)], axis=0)
            bias = bias_ref[pl.ds(pl.multiple_of(tile * 16, 16), 16), quad * 256 : quad * 256 + 256]
            return held, dot_t(query, held) + jnp.concatenate([bias] * HEADS, axis=0)

        def soften(held, scores):
            raised = jnp.exp2(scores - jnp.max(scores, axis=1, keepdims=True)).astype(BF)
            return held, raised

        def gather(held, raised):
            return dot(raised, jnp.concatenate([held, ones], axis=1))

        def finish(i, summed):
            t, b, a = i // 4, i // 2 % 2, i % 2
            quad = 2 * a + b
            part = summed[:, :128] / summed[:, 128:]
            joined = [
                jnp.where(low_lane, part[32 * k : 32 * k + 16], part[32 * k + 16 : 32 * k + 32])
                for k in range(HEADS // 2)
            ]
            u_ref[pl.ds(t * 64 + quad * 16, 16), :] = jnp.concatenate(joined, axis=1).astype(BF)

        count = GROUP * 4
        scored, softened, gathered = {}, {}, {}
        for i in range(count + LAG3):
            if i < count:
                scored[i] = start(i)
            if i % 4 == OUT_AT and i < count:
                project(i // 4)
            j = i - LAG1
            if 0 <= j < count:
                softened[j] = soften(*scored.pop(j))
            j = i - LAG2
            if 0 <= j < count:
                gathered[j] = gather(*softened.pop(j))
            j = i - LAG3
            if 0 <= j < count:
                finish(j, gathered.pop(j))

        @pl.when(step >= 1)
        def _():
            copy_out(step - 1).start()

        return carry

    u_ref[...] = jnp.zeros(u_ref.shape, BF)
    lax.fori_loop(0, last, body, 0)
    copy_out(last - 3).wait()
    place()
    for n in range(0, D, 512):
        made_ref[(last - 1) % 2, :, n : n + 512] = dot(placed_ref[...], out_mix_ref[:, n : n + 512]).astype(BF)
    copy_out(last - 1).start()
    copy_out(last - 2).wait()
    copy_out(last - 1).wait()


def attend(owner, slot, z, q, out_mix, fixed):
    smem = pl.BlockSpec(memory_space=pltpu.SMEM)
    vmem = pl.BlockSpec(memory_space=pltpu.VMEM)
    rows = GROUP * 64
    return pl.pallas_call(
        attend_kernel,
        out_shape=jax.ShapeDtypeStruct((TILES * 64, D), BF),
        in_specs=[smem, smem] + [vmem] * 4,
        out_specs=pl.BlockSpec(memory_space=pl.ANY),
        scratch_shapes=[
            pltpu.VMEM((rows, HEADS * LAT), BF),
            pltpu.VMEM((TILES * 16, 1024), F32),
            pltpu.VMEM((rows, HEADS * LAT), BF),
            pltpu.VMEM((2, rows, D), BF),
            pltpu.SemaphoreType.DMA((2,)),
        ],
        compiler_params=pltpu.CompilerParams(vmem_limit_bytes=24 * 2**20),
        cost_estimate=pl.CostEstimate(flops=8 * 10**9, bytes_accessed=10**7, transcendentals=3 * 10**6),
        name="attend",
    )(owner.T, slot.T, z, q, out_mix, fixed)


CHUNK = 512
MESH = pl.DeviceIdType.MESH


def route_kernel(
    owner_in, latents_ref, embed_in, gain_in, wq_ref, wk_ref, wv_ref, wo_ref,
    moving_in,
    z_ref, q_ref, out_mix_ref,
    latents, wq, wk, wv, wo, owner_ref, embed_ref, gain_ref, moving, mix_ref, stage, outbox, inbox, ext, sems, local_sems,
    send_sem, recv_sem, halo_send, halo_recv,
):
    devices = lax.axis_size("tile")
    me = lax.axis_index("tile")
    edge = HALO * 32

    def load(index, source, target):
        copy = pltpu.make_async_copy(source, target, local_sems.at[index])
        copy.start()
        return copy

    owners = load(0, owner_in, owner_ref)
    loading = load(1, latents_ref, latents)
    parameters = [load(2, embed_in, embed_ref), load(3, gain_in, gain_ref), load(4, moving_in, moving)]
    copies = []
    for w, (source, target) in enumerate(((wq_ref, wq), (wk_ref, wk), (wv_ref, wv), (wo_ref, wo))):
        row_count = source.shape[0] // 4
        for c in range(4):
            cut = pl.ds(c * row_count, row_count)
            copy = pltpu.make_async_copy(source.at[cut], target.at[cut], sems.at[w, c])
            copy.start()
            copies.append(copy)

    barrier = pltpu.get_barrier_semaphore()

    def greet(k, carry):
        pl.semaphore_signal(barrier, inc=1, device_id={"tile": lax.rem(me + k, devices)}, device_id_type=MESH)
        return carry

    lax.fori_loop(1, devices, greet, 0)

    owners.wait()
    slots = owner_ref.shape[0]
    live = lax.fori_loop(0, slots, lambda j, n: n + jnp.where(owner_ref[j] >= 0, 1, 0), 0)
    dest = lax.broadcasted_iota(jnp.int32, (devices, slots), 0)
    slot = lax.broadcasted_iota(jnp.int32, (devices, slots), 1)
    first = owner_ref[0]
    chosen = jnp.where(((dest - first) % devices == slot) & (slot < live), 1.0, 0.0).astype(BF)
    row = lax.broadcasted_iota(jnp.int32, (devices, 128), 0)
    dead = jnp.where((row - first) % devices < live, 0.0, 512.0)
    loading.wait()
    for n in range(0, TILE_VALUES, 512):
        made = dot(chosen, latents[:, n : n + 512])
        for k in range(4):
            stage[pl.ds(n // 128 + k, devices, stride=32), :] = made[:, k * 128 : k * 128 + 128] + dead

    def pack(d, carry):
        outbox[d] = stage[pl.ds(pl.multiple_of(d * 32, 32), 32), :].astype(BF)
        return carry

    lax.fori_loop(0, devices, pack, 0)
    inbox[me] = outbox[me]
    pl.semaphore_wait(barrier, devices - 1)

    def send(k, carry):
        target = lax.rem(me + k, devices)
        pltpu.make_async_remote_copy(
            src_ref=outbox.at[target], dst_ref=inbox.at[me], send_sem=send_sem, recv_sem=recv_sem,
            device_id={"tile": target}, device_id_type=MESH,
        ).start()
        return carry

    lax.fori_loop(1, devices, send, 0)

    for copy in parameters:
        copy.wait()
    embed = embed_ref[...]
    scaled = embed.astype(F32) * gain_ref[...]
    stacked = jnp.concatenate(split(scaled), axis=0)
    twice = jnp.concatenate([embed, embed], axis=0)
    same = lax.broadcasted_iota(jnp.int32, (128, 128), 0) // LAT == lax.broadcasted_iota(jnp.int32, (128, 128), 1) // LAT
    gram = jnp.concatenate(split(jnp.where(same, dot_t(twice, twice) * (1.0 / D), 0.0)), axis=1)
    block = jnp.where(same, 1.0, 0.0).astype(BF)
    block = jnp.concatenate([block, block], axis=0)

    def folded(w, held):
        total = jnp.zeros((2 * LAT, HEADS * HEAD), F32)
        for c in range(4):
            copies[w * 4 + c].wait()
            total += dot(stacked[:, c * CHUNK : (c + 1) * CHUNK], held[pl.ds(c * CHUNK, CHUNK), :])
        return split(total[:LAT] + total[LAT:])

    query_high, query_low = folded(0, wq)
    key_high, key_low = folded(1, wk)
    for h in range(HEADS):
        cut = slice(h * HEAD, (h + 1) * HEAD)
        left = jnp.concatenate([query_high[:, cut], query_low[:, cut], query_high[:, cut]], axis=1)
        right = jnp.concatenate([key_high[:, cut], key_high[:, cut], key_low[:, cut]], axis=1)
        high, low = split(dot_t(left, jnp.concatenate([right, right], axis=0)) * SCALE)
        mix_ref[:, cut] = jnp.concatenate([high, high, low, low], axis=0)
    value = jnp.concatenate(folded(2, wv), axis=0)

    for h in range(HEADS):
        cut = slice(h * HEAD, (h + 1) * HEAD)
        if h % 2 == 0:
            copies[12 + h // 2].wait()
        for n in range(0, D, 512):
            made = dot(value[:, cut], wo[cut, n : n + 512])
            out_mix_ref[pl.ds(h * LAT, LAT), n : n + 512] = (made[:LAT] + made[LAT:]).astype(BF)

    everyone = pltpu.make_async_remote_copy(
        src_ref=outbox.at[pl.ds(0, devices - 1)], dst_ref=inbox.at[pl.ds(0, devices - 1)],
        send_sem=send_sem, recv_sem=recv_sem, device_id={"tile": lax.rem(me + 1, devices)}, device_id_type=MESH,
    )
    everyone.wait_recv()

    lane = lax.broadcasted_iota(jnp.int32, (8, 128), 1)

    def rank(source, carry):
        seen, places = carry
        lives = inbox[source, 0:16, :].astype(F32)[:8] < 100.0
        seen = seen + jnp.where(lives, 1, 0)
        return seen, places + jnp.where(seen <= lane, 1, 0)

    zero = jnp.zeros((8, 128), jnp.int32)
    _, places = lax.fori_loop(0, devices, rank, (zero, zero))
    for p in range(TILES):
        ext[pl.ds(edge + p * 32, 32), :] = inbox[jnp.minimum(places[0, p], devices - 1)]
    mine = pl.ds(edge, TILES * 32)
    held = ext[mine, :]
    tall = dot(held, gram)
    wide = held.astype(F32)
    mean = dot(jnp.concatenate(split((tall[:, :128] + tall[:, 128:]) * wide), axis=1), block)
    ext[mine, :] = (wide * lax.rsqrt(jnp.maximum(mean, 0.0) + EPSILON)).astype(BF)

    halos = []
    for side, (start, end, step) in enumerate(((TILES * 32, 0, 1), (edge, edge + TILES * 32, devices - 1))):
        copy = pltpu.make_async_remote_copy(
            src_ref=ext.at[pl.ds(start, edge)], dst_ref=ext.at[pl.ds(end, edge)],
            send_sem=halo_send.at[side], recv_sem=halo_recv.at[side],
            device_id={"tile": lax.rem(me + step, devices)}, device_id_type=MESH,
        )
        copy.start()
        halos.append(copy)

    rows = GROUP * 32
    order = moving[pl.ds(768, 256), :]
    double = jnp.concatenate([moving[0:128, :], moving[128:256, :]], axis=1)
    spread = moving[pl.ds(256, 512), :]
    parity = (lax.broadcasted_iota(jnp.int32, (GROUP * 64, 128), 0) // 8) % 2
    half = lax.broadcasted_iota(jnp.int32, (GROUP * 64, 128), 1) // LAT
    keep = (parity == half).astype(F32)
    for g in range(TILES // GROUP):
        picked = (dot(order, ext[pl.ds(edge + g * rows, rows), :]) * keep).astype(BF)
        both = jnp.concatenate([picked, picked], axis=1)
        q_ref[pl.ds(g * GROUP * 64, GROUP * 64), :] = dot(both, mix_ref[...]).astype(BF)

    def spread_out(first):
        pair = dot(ext[pl.ds(first * 32, rows), :], double).astype(BF)
        made = dot(spread, pair).astype(BF)
        for p in range(2):
            z_ref[p, pl.ds(first * 128, GROUP * 128), :] = made[:, p * 128 : p * 128 + 128]

    for g in range(TILES // GROUP):
        spread_out(HALO + g * GROUP)
    everyone.wait_send()
    for copy in halos:
        copy.wait()
    for start in (0, HALO + TILES):
        for first in (0, 4, 8, HALO - GROUP):
            spread_out(start + first)


def route(tile_owner, tile_latents, w_embed, norm_gain, w_query, w_key, w_value, w_out, moving):
    devices = lax.axis_size("tile")
    vmem = pl.BlockSpec(memory_space=pltpu.VMEM)
    hbm = pl.BlockSpec(memory_space=pltpu.HBM)
    dma = pltpu.SemaphoreType.DMA
    return pl.pallas_call(
        route_kernel,
        out_shape=(
            jax.ShapeDtypeStruct((2, EXT * 128, 128), BF),
            jax.ShapeDtypeStruct((TILES * 64, HEADS * HEAD), BF),
            jax.ShapeDtypeStruct((HEADS * LAT, D), BF),
        ),
        in_specs=[hbm] * 9,
        out_specs=(vmem, vmem, vmem),
        scratch_shapes=[pltpu.VMEM(tile_latents.shape, BF)]
        + [pltpu.VMEM(w.shape, BF) for w in (w_query, w_key, w_value, w_out)]
        + [
            pltpu.SMEM(tile_owner.shape, jnp.int32),
            pltpu.VMEM(w_embed.shape, BF),
            pltpu.VMEM((1, D), F32),
            pltpu.VMEM(moving.shape, BF),
            pltpu.VMEM((4 * LAT, HEADS * HEAD), BF),
            pltpu.VMEM((devices * 32, 128), F32),
            pltpu.VMEM((devices, 32, 128), BF),
            pltpu.VMEM((devices, 32, 128), BF),
            pltpu.VMEM((EXT * 32, 128), BF),
            dma((4, 4)), dma((5,)), dma, dma, dma((2,)), dma((2,)),
        ],
        compiler_params=pltpu.CompilerParams(
            vmem_limit_bytes=40 * 2**20, collective_id=0, has_side_effects=True
        ),
        cost_estimate=pl.CostEstimate(flops=3 * 10**9, bytes_accessed=2 * 10**7, transcendentals=0),
        name="route",
    )(
        *[
            pltpu.with_memory_space_constraint(x, pltpu.HBM)
            for x in (
                tile_owner, tile_latents, w_embed, norm_gain.reshape(1, D), w_query, w_key, w_value, w_out, moving,
            )
        ],
    )


def local(
    tile_latents, tile_owner, tile_position, neighbour_owner, neighbour_slot,
    w_embed, norm_gain, w_query, w_key, w_value, w_out,
):
    moving, fixed = (jnp.asarray(c) for c in place_constants())
    z, q, out_mix = route(tile_owner, tile_latents, w_embed, norm_gain, w_query, w_key, w_value, w_out, moving)
    return attend(neighbour_owner, neighbour_slot, z, q, out_mix, fixed)


def solution(mesh):
    both = P(("dp", "tile"), None)
    flat = P(("dp", "tile"))
    return jax.shard_map(
        local,
        mesh=mesh,
        in_specs=(both, flat, flat, both, both, P(), P(), P(), P(), P(), P()),
        out_specs=both,
        check_vma=False,
    )
```

```python
import math

import jax
import jax.numpy as jnp
import numpy as np
from jax import lax
from jax.experimental import pallas as pl
from jax.experimental.pallas import tpu as pltpu
from jax.sharding import PartitionSpec as P

D = 2048
HEADS = 8
HEAD = 128
LAT = 64
SIDE = 8
RADIUS = 6
HALO = 14
TILES = 24
TILE_VALUES = 4096
EXT = TILES + 2 * HALO
EPSILON = 1e-06
AWAY = -1e38
GROUP = 4
SCALE = 0.5 * HEAD ** -0.5 * math.log2(math.e)

BF = jnp.bfloat16
F32 = jnp.float32


def place_constants():
    double = np.zeros((2, LAT, 2, 2, LAT), np.float32)
    for p in range(2):
        for k in range(LAT):
            double[p, k, p, :, k] = 1
    double = double.reshape(128, 256)
    spread = np.zeros((GROUP, 2, 8, 8, GROUP, 8, 4), np.float32)
    for t in range(GROUP):
        for form in range(2):
            for r in range(8):
                for s in range(8):
                    spread[t, form, r, s, t, r, (s + 1 + 2 * form) % 4] = 1
    spread = spread.reshape(GROUP * 128, GROUP * 32)
    order = np.zeros((GROUP, 2, 2, 2, 4, 2, GROUP, 8, 4), np.float32)
    back = np.zeros((GROUP, 8, 8, GROUP, 2, 2, 2, 4, 2), np.float32)
    for t in range(GROUP):
        for a in range(2):
            for b in range(2):
                for p in range(2):
                    for r in range(4):
                        for c in range(2):
                            order[t, a, b, p, r, c, t, 4 * a + r, 2 * b + c] = 1
                            back[t, 4 * a + r, 4 * b + 2 * c + p, t, a, b, p, r, c] = 1
    order = order.reshape(GROUP * 64, GROUP * 32)
    back = back.reshape(GROUP * 64, GROUP * 64)
    query_extra = np.zeros((2, 4, 2, 128), np.float32)
    for p in range(2):
        for r in range(4):
            for c in range(2):
                query_extra[p, r, c, 8 + r] = 1
                query_extra[p, r, c, 12 + 2 * c + p] = 1
    query_extra = query_extra.reshape(16, 128)
    key_extra = np.zeros((2, 2, 2, 16, 8, 128), np.float32)
    for a in range(2):
        for b in range(2):
            for p in range(2):
                for row in range(16):
                    for s in range(8):
                        col = 2 * s + p
                        tile_row = (4 * a - 6 + row) // 8 + 1
                        tile_col = (4 * b - 6 + col) // 8 + 1
                        region = tile_row * 3 + tile_col
                        lane = key_extra[a, b, p, row, s]
                        if region != 4:
                            lane[region - (region > 4)] = 1
                        for i in range(4):
                            lane[8 + i] = 0 if i <= row <= i + 2 * RADIUS else AWAY
                            lane[12 + i] = 0 if i <= col <= i + 2 * RADIUS else AWAY
    key_extra = key_extra.reshape(1024, 128)
    stack = lambda x: np.concatenate([x[:, :128], x[:, 128:]], axis=0)
    moving = np.concatenate([stack(double), spread, order, query_extra, key_extra], axis=0).astype(jnp.bfloat16)
    fixed = stack(back).astype(jnp.bfloat16)
    return moving, fixed


def split(x):
    high = x.astype(BF)
    low = (x - high.astype(F32)).astype(BF)
    return high, low


def dot(a, b):
    return jnp.dot(a, b, preferred_element_type=F32)


def dot_t(a, b):
    return lax.dot_general(a, b, (((1,), (1,)), ((), ())), preferred_element_type=F32)


LAG1, LAG2, LAG3 = 2, 4, 6
OUT_AT = 3


def attend_kernel(
    owner_ref, slot_ref, z_ref, q_ref, bias_ref, out_mix_ref, fixed_ref, out_ref, u_ref, placed_ref, made_ref, sems, piece_sems,
):
    me = lax.axis_index("tile")
    low_lane = lax.broadcasted_iota(jnp.int32, (16, 128), 1) < LAT

    sub = lax.broadcasted_iota(jnp.int32, (16, 128), 0) % 8
    ones = jnp.ones((256, 128), BF)

    rows = GROUP * 64
    last = TILES // GROUP

    def place():
        placed_ref[...] = dot(jnp.concatenate([fixed_ref[0:256, :], fixed_ref[256:512, :]], axis=1), u_ref[...]).astype(BF)

    def copy_out(g):
        slot = g % 2
        return pltpu.make_async_copy(
            made_ref.at[slot], out_ref.at[pl.ds(pl.multiple_of(g * rows, rows), rows)], sems.at[slot]
        )

    def body(step, carry):
        @pl.when(step >= 3)
        def _():
            copy_out(step - 3).wait()

        place()
        slot = (step + 1) % 2

        def project(n):
            made_ref[slot, :, n * 512 : n * 512 + 512] = dot(
                placed_ref[...], out_mix_ref[:, n * 512 : n * 512 + 512]
            ).astype(BF)

        def region(t):
            tile = step * GROUP + t
            places = []
            for n in range(8):
                owner = owner_ref[n, tile]
                place = HALO + (owner - me) * TILES + slot_ref[n, tile]
                places.append(jnp.where(owner >= 0, place, HALO + tile))
            places = places[:4] + [HALO + tile] + places[4:]
            return tile, [p * 128 for p in places]

        def window(bases, b):
            first, last = ((3, 7), (1, 5))[b]
            sides = []
            for p in range(2):
                strips = []
                for tile_row, pairs in ((0, (1, 2, 3)), (1, (0, 1, 2, 3)), (2, (0, 1, 2))):
                    for pair in pairs:
                        left, mid, right = (
                            z_ref[p, pl.ds(pl.multiple_of(bases[tile_row * 3 + k] + b * 64 + pair * 16, 16), 16), :]
                            for k in range(3)
                        )
                        strips.append(jnp.where(sub < first, left, jnp.where(sub < last, mid, right)))
                sides.append(strips)
            return sides

        work = {}

        def start(i):
            t, b, a = i // 4, i // 2 % 2, i % 2
            quad = 2 * a + b
            if i % 4 == 0:
                work["region"] = region(t)
            tile, bases = work["region"]
            if a == 0:
                work["window"] = window(bases, b)
            even, odd = work["window"]
            cut = slice(2 * a, 2 * a + 8)
            held = jnp.concatenate(even[cut] + odd[cut], axis=0)
            block = q_ref[pl.ds(pl.multiple_of(tile * 64 + quad * 16, 16), 16), :]
            query = jnp.concatenate([block[:, h * 128 : h * 128 + 128] for h in range(HEADS)], axis=0)
            bias = bias_ref[pl.ds(pl.multiple_of(tile * 16, 16), 16), quad * 256 : quad * 256 + 256]
            return held, dot_t(query, held) + jnp.concatenate([bias] * HEADS, axis=0)

        def soften(held, scores):
            raised = jnp.exp2(scores - jnp.max(scores, axis=1, keepdims=True)).astype(BF)
            return held, raised

        def gather(held, raised):
            return dot(raised, jnp.concatenate([held, ones], axis=1))

        def finish(i, summed):
            t, b, a = i // 4, i // 2 % 2, i % 2
            quad = 2 * a + b
            part = summed[:, :128] / summed[:, 128:]
            joined = [
                jnp.where(low_lane, part[32 * k : 32 * k + 16], part[32 * k + 16 : 32 * k + 32])
                for k in range(HEADS // 2)
            ]
            u_ref[pl.ds(t * 64 + quad * 16, 16), :] = jnp.concatenate(joined, axis=1).astype(BF)

        count = GROUP * 4
        scored, softened, gathered = {}, {}, {}
        for i in range(count + LAG3):
            if i < count:
                scored[i] = start(i)
            if i % 4 == OUT_AT and i < count:
                project(i // 4)
            j = i - LAG1
            if 0 <= j < count:
                softened[j] = soften(*scored.pop(j))
            j = i - LAG2
            if 0 <= j < count:
                gathered[j] = gather(*softened.pop(j))
            j = i - LAG3
            if 0 <= j < count:
                finish(j, gathered.pop(j))

        @pl.when(step >= 1)
        def _():
            copy_out(step - 1).start()

        return carry

    u_ref[...] = jnp.zeros(u_ref.shape, BF)
    lax.fori_loop(0, last, body, 0)
    copy_out(last - 3).wait()
    place()
    pieces = []
    for k in range(4):
        cut = slice(k * 512, k * 512 + 512)
        made_ref[(last - 1) % 2, :, cut] = dot(placed_ref[...], out_mix_ref[:, cut]).astype(BF)
        piece = pltpu.make_async_copy(
            made_ref.at[(last - 1) % 2, :, pl.ds(k * 512, 512)],
            out_ref.at[pl.ds((last - 1) * rows, rows), pl.ds(k * 512, 512)], piece_sems.at[k],
        )
        piece.start()
        pieces.append(piece)
    copy_out(last - 2).wait()
    for piece in pieces:
        piece.wait()


def attend(owner, slot, z, q, bias, out_mix, fixed):
    smem = pl.BlockSpec(memory_space=pltpu.SMEM)
    vmem = pl.BlockSpec(memory_space=pltpu.VMEM)
    rows = GROUP * 64
    return pl.pallas_call(
        attend_kernel,
        out_shape=jax.ShapeDtypeStruct((TILES * 64, D), BF),
        in_specs=[smem, smem] + [vmem] * 5,
        out_specs=pl.BlockSpec(memory_space=pl.ANY),
        scratch_shapes=[
            pltpu.VMEM((rows, HEADS * LAT), BF),
            pltpu.VMEM((rows, HEADS * LAT), BF),
            pltpu.VMEM((2, rows, D), BF),
            pltpu.SemaphoreType.DMA((2,)),
            pltpu.SemaphoreType.DMA((4,)),
        ],
        compiler_params=pltpu.CompilerParams(vmem_limit_bytes=24 * 2**20),
        cost_estimate=pl.CostEstimate(flops=8 * 10**9, bytes_accessed=10**7, transcendentals=3 * 10**6),
        name="attend",
    )(owner.T, slot.T, z, q, bias, out_mix, fixed)


CHUNK = 512
MESH = pl.DeviceIdType.MESH


def route_kernel(
    owner_in, latents_ref, embed_in, gain_in, wq_ref, wk_ref, wv_ref, wo_ref,
    moving_in, around_in,
    z_ref, q_ref, bias_ref, out_mix_ref,
    latents, wq, wk, wv, wo, owner_ref, embed_ref, gain_ref, moving, around, mix_ref, stage, outbox, inbox, ext, sems, local_sems,
    send_sem, recv_sem, halo_send, halo_recv,
):
    devices = lax.axis_size("tile")
    me = lax.axis_index("tile")
    edge = HALO * 32

    def load(index, source, target):
        copy = pltpu.make_async_copy(source, target, local_sems.at[index])
        copy.start()
        return copy

    owners = load(0, owner_in, owner_ref)
    loading = load(1, latents_ref, latents)

    barrier = pltpu.get_barrier_semaphore()

    def greet(k, carry):
        pl.semaphore_signal(barrier, inc=1, device_id={"tile": lax.rem(me + k, devices)}, device_id_type=MESH)
        return carry

    lax.fori_loop(1, devices, greet, 0)

    parameters = [load(2, embed_in, embed_ref), load(3, gain_in, gain_ref), load(4, moving_in, moving), load(5, around_in, around)]
    copies = []
    for w, (source, target) in enumerate(((wq_ref, wq), (wk_ref, wk), (wv_ref, wv), (wo_ref, wo))):
        row_count = source.shape[0] // 4
        for c in range(4):
            cut = pl.ds(c * row_count, row_count)
            copy = pltpu.make_async_copy(source.at[cut], target.at[cut], sems.at[w, c])
            copy.start()
            copies.append(copy)

    owners.wait()
    slots = owner_ref.shape[0]
    live = lax.fori_loop(0, slots, lambda j, n: n + jnp.where(owner_ref[j] >= 0, 1, 0), 0)
    dest = lax.broadcasted_iota(jnp.int32, (devices, slots), 0)
    slot = lax.broadcasted_iota(jnp.int32, (devices, slots), 1)
    first = owner_ref[0]
    chosen = jnp.where(((dest - first) % devices == slot) & (slot < live), 1.0, 0.0).astype(BF)
    row = lax.broadcasted_iota(jnp.int32, (devices, 128), 0)
    dead = jnp.where((row - first) % devices < live, 0.0, 512.0)
    loading.wait()
    for n in range(0, TILE_VALUES, 512):
        made = dot(chosen, latents[:, n : n + 512])
        for k in range(4):
            stage[pl.ds(n // 128 + k, devices, stride=32), :] = made[:, k * 128 : k * 128 + 128] + dead

    def pack(d, carry):
        outbox[d] = stage[pl.ds(pl.multiple_of(d * 32, 32), 32), :].astype(BF)
        return carry

    lax.fori_loop(0, devices, pack, 0, unroll=8)
    inbox[me] = outbox[me]
    pl.semaphore_wait(barrier, devices - 1)

    def send(k, carry):
        target = lax.rem(me + k, devices)
        pltpu.make_async_remote_copy(
            src_ref=outbox.at[target], dst_ref=inbox.at[me], send_sem=send_sem, recv_sem=recv_sem,
            device_id={"tile": target}, device_id_type=MESH,
        ).start()
        return carry

    lax.fori_loop(1, devices, send, 0)

    for copy in parameters:
        copy.wait()
    embed = embed_ref[...]
    scaled = embed.astype(F32) * gain_ref[...]
    stacked = jnp.concatenate(split(scaled), axis=0)
    twice = jnp.concatenate([embed, embed], axis=0)
    same = lax.broadcasted_iota(jnp.int32, (128, 128), 0) // LAT == lax.broadcasted_iota(jnp.int32, (128, 128), 1) // LAT
    gram = jnp.concatenate(split(jnp.where(same, dot_t(twice, twice) * (1.0 / D), 0.0)), axis=1)
    block = jnp.where(same, 1.0, 0.0).astype(BF)
    block = jnp.concatenate([block, block], axis=0)

    def folded(w, held):
        total = jnp.zeros((2 * LAT, HEADS * HEAD), F32)
        for c in range(4):
            copies[w * 4 + c].wait()
            total += dot(stacked[:, c * CHUNK : (c + 1) * CHUNK], held[pl.ds(c * CHUNK, CHUNK), :])
        return split(total[:LAT] + total[LAT:])

    query_high, query_low = folded(0, wq)
    key_high, key_low = folded(1, wk)
    for h in range(HEADS):
        cut = slice(h * HEAD, (h + 1) * HEAD)
        left = jnp.concatenate([query_high[:, cut], query_low[:, cut], query_high[:, cut]], axis=1)
        right = jnp.concatenate([key_high[:, cut], key_high[:, cut], key_low[:, cut]], axis=1)
        high, low = split(dot_t(left, jnp.concatenate([right, right], axis=0)) * SCALE)
        mix_ref[:, cut] = jnp.concatenate([high, high, low, low], axis=0)
    value = jnp.concatenate(folded(2, wv), axis=0)

    for h in range(HEADS):
        cut = slice(h * HEAD, (h + 1) * HEAD)
        if h % 2 == 0:
            copies[12 + h // 2].wait()
        for n in range(0, D, 512):
            made = dot(value[:, cut], wo[cut, n : n + 512])
            out_mix_ref[pl.ds(h * LAT, LAT), n : n + 512] = (made[:LAT] + made[LAT:]).astype(BF)

    extra_lane = lax.broadcasted_iota(jnp.int32, (16, 128), 1)
    sides = []
    for t in range(TILES):
        side = moving[pl.ds(1024, 16), :].astype(F32)
        for n in range(8):
            side = jnp.where(extra_lane == n, jnp.where(around[n, t] >= 0, 0.0, AWAY).astype(F32), side)
        sides.append(side.astype(BF))
    bias_ref[...] = dot_t(jnp.concatenate(sides, axis=0), moving[pl.ds(1040, 1024), :])
    everyone = pltpu.make_async_remote_copy(
        src_ref=outbox.at[pl.ds(0, devices - 1)], dst_ref=inbox.at[pl.ds(0, devices - 1)],
        send_sem=send_sem, recv_sem=recv_sem, device_id={"tile": lax.rem(me + 1, devices)}, device_id_type=MESH,
    )
    everyone.wait_recv()

    lane = lax.broadcasted_iota(jnp.int32, (8, 128), 1)

    def rank(source, carry):
        seen, places = carry
        lives = inbox[source, 0:16, :].astype(F32)[:8] < 100.0
        seen = seen + jnp.where(lives, 1, 0)
        return seen, places + jnp.where(seen <= lane, 1, 0)

    zero = jnp.zeros((8, 128), jnp.int32)
    _, places = lax.fori_loop(0, devices, rank, (zero, zero), unroll=8)
    for p in range(TILES):
        ext[pl.ds(edge + p * 32, 32), :] = inbox[jnp.minimum(places[0, p], devices - 1)]
    mine = pl.ds(edge, TILES * 32)
    held = ext[mine, :]
    tall = dot(held, gram)
    wide = held.astype(F32)
    mean = dot(jnp.concatenate(split((tall[:, :128] + tall[:, 128:]) * wide), axis=1), block)
    ext[mine, :] = (wide * lax.rsqrt(jnp.maximum(mean, 0.0) + EPSILON)).astype(BF)

    last = devices - 1

    def halo(side):
        start, end, partner = ((TILES * 32, 0, me + 1), (edge, edge + TILES * 32, me - 1))[side]
        return pltpu.make_async_remote_copy(
            src_ref=ext.at[pl.ds(start, edge)], dst_ref=ext.at[pl.ds(end, edge)],
            send_sem=halo_send.at[side], recv_sem=halo_recv.at[side],
            device_id={"tile": lax.rem(partner + devices, devices)}, device_id_type=MESH,
        )

    @pl.when(me < last)
    def _():
        halo(0).start()

    @pl.when(me > 0)
    def _():
        halo(1).start()

    @pl.when(me == 0)
    def _():
        ext[pl.ds(0, edge), :] = jnp.zeros((edge, 128), BF)

    @pl.when(me == last)
    def _():
        ext[pl.ds(edge + TILES * 32, edge), :] = jnp.zeros((edge, 128), BF)

    rows = GROUP * 32
    order = moving[pl.ds(768, 256), :]
    double = jnp.concatenate([moving[0:128, :], moving[128:256, :]], axis=1)
    spread = moving[pl.ds(256, 512), :]
    parity = (lax.broadcasted_iota(jnp.int32, (GROUP * 64, 128), 0) // 8) % 2
    half = lax.broadcasted_iota(jnp.int32, (GROUP * 64, 128), 1) // LAT
    keep = (parity == half).astype(F32)
    for g in range(TILES // GROUP):
        picked = (dot(order, ext[pl.ds(edge + g * rows, rows), :]) * keep).astype(BF)
        both = jnp.concatenate([picked, picked], axis=1)
        q_ref[pl.ds(g * GROUP * 64, GROUP * 64), :] = dot(both, mix_ref[...]).astype(BF)

    def spread_out(first):
        pair = dot(ext[pl.ds(first * 32, rows), :], double).astype(BF)
        made = dot(spread, pair).astype(BF)
        for p in range(2):
            z_ref[p, pl.ds(first * 128, GROUP * 128), :] = made[:, p * 128 : p * 128 + 128]

    for g in range(TILES // GROUP):
        spread_out(HALO + g * GROUP)
    everyone.wait_send()

    @pl.when(me < last)
    def _():
        halo(0).wait_send()
        halo(1).wait_recv()

    @pl.when(me > 0)
    def _():
        halo(1).wait_send()
        halo(0).wait_recv()

    for start in (0, HALO + TILES):
        for first in (0, 4, 8, HALO - GROUP):
            spread_out(start + first)


def route(tile_owner, tile_latents, w_embed, norm_gain, w_query, w_key, w_value, w_out, moving, around):
    devices = lax.axis_size("tile")
    vmem = pl.BlockSpec(memory_space=pltpu.VMEM)
    hbm = pl.BlockSpec(memory_space=pltpu.HBM)
    dma = pltpu.SemaphoreType.DMA
    return pl.pallas_call(
        route_kernel,
        out_shape=(
            jax.ShapeDtypeStruct((2, EXT * 128, 128), BF),
            jax.ShapeDtypeStruct((TILES * 64, HEADS * HEAD), BF),
            jax.ShapeDtypeStruct((TILES * 16, 1024), F32),
            jax.ShapeDtypeStruct((HEADS * LAT, D), BF),
        ),
        in_specs=[hbm] * 10,
        out_specs=(vmem, vmem, vmem, vmem),
        scratch_shapes=[pltpu.VMEM(tile_latents.shape, BF)]
        + [pltpu.VMEM(w.shape, BF) for w in (w_query, w_key, w_value, w_out)]
        + [
            pltpu.SMEM(tile_owner.shape, jnp.int32),
            pltpu.VMEM(w_embed.shape, BF),
            pltpu.VMEM((1, D), F32),
            pltpu.VMEM(moving.shape, BF),
            pltpu.SMEM(around.shape, jnp.int32),
            pltpu.VMEM((4 * LAT, HEADS * HEAD), BF),
            pltpu.VMEM((devices * 32, 128), F32),
            pltpu.VMEM((devices, 32, 128), BF),
            pltpu.VMEM((devices, 32, 128), BF),
            pltpu.VMEM((EXT * 32, 128), BF),
            dma((4, 4)), dma((6,)), dma, dma, dma((2,)), dma((2,)),
        ],
        compiler_params=pltpu.CompilerParams(
            vmem_limit_bytes=40 * 2**20, collective_id=0, has_side_effects=True
        ),
        cost_estimate=pl.CostEstimate(flops=3 * 10**9, bytes_accessed=2 * 10**7, transcendentals=0),
        name="route",
    )(
        *[
            pltpu.with_memory_space_constraint(x, pltpu.HBM)
            for x in (
                tile_owner, tile_latents, w_embed, norm_gain.reshape(1, D), w_query, w_key, w_value, w_out, moving,
                around,
            )
        ],
    )


def local(
    tile_latents, tile_owner, tile_position, neighbour_owner, neighbour_slot,
    w_embed, norm_gain, w_query, w_key, w_value, w_out,
):
    moving, fixed = (jnp.asarray(c) for c in place_constants())
    z, q, bias, out_mix = route(
        tile_owner, tile_latents, w_embed, norm_gain, w_query, w_key, w_value, w_out, moving, neighbour_owner.T
    )
    return attend(neighbour_owner, neighbour_slot, z, q, bias, out_mix, fixed)


def solution(mesh):
    both = P(("dp", "tile"), None)
    flat = P(("dp", "tile"))
    return jax.shard_map(
        local,
        mesh=mesh,
        in_specs=(both, flat, flat, both, both, P(), P(), P(), P(), P(), P()),
        out_specs=both,
        check_vma=False,
    )
```

```python
import math

import jax
import jax.numpy as jnp
import numpy as np
from jax import lax
from jax.experimental import pallas as pl
from jax.experimental.pallas import tpu as pltpu
from jax.sharding import PartitionSpec as P

D = 2048
HEADS = 8
HEAD = 128
LAT = 64
SIDE = 8
RADIUS = 6
HALO = 14
TILES = 24
TILE_VALUES = 4096
EXT = TILES + 2 * HALO
EPSILON = 1e-06
AWAY = -1e38
GROUP = 4
SCALE = 0.5 * HEAD ** -0.5 * math.log2(math.e)

BF = jnp.bfloat16
F32 = jnp.float32


def place_constants():
    double = np.zeros((2, LAT, 2, 2, LAT), np.float32)
    for p in range(2):
        for k in range(LAT):
            double[p, k, p, :, k] = 1
    double = double.reshape(128, 256)
    spread = np.zeros((GROUP, 2, 8, 8, GROUP, 8, 4), np.float32)
    for t in range(GROUP):
        for form in range(2):
            for r in range(8):
                for s in range(8):
                    spread[t, form, r, s, t, r, (s + 1 + 2 * form) % 4] = 1
    spread = spread.reshape(GROUP * 128, GROUP * 32)
    order = np.zeros((GROUP, 2, 2, 2, 4, 2, GROUP, 8, 4), np.float32)
    back = np.zeros((GROUP, 8, 8, GROUP, 2, 2, 2, 4, 2), np.float32)
    for t in range(GROUP):
        for a in range(2):
            for b in range(2):
                for p in range(2):
                    for r in range(4):
                        for c in range(2):
                            order[t, a, b, p, r, c, t, 4 * a + r, 2 * b + c] = 1
                            back[t, 4 * a + r, 4 * b + 2 * c + p, t, a, b, p, r, c] = 1
    order = order.reshape(GROUP * 64, GROUP * 32)
    back = back.reshape(GROUP * 64, GROUP * 64)
    query_extra = np.zeros((2, 4, 2, 128), np.float32)
    for p in range(2):
        for r in range(4):
            for c in range(2):
                query_extra[p, r, c, 8 + r] = 1
                query_extra[p, r, c, 12 + 2 * c + p] = 1
    query_extra = query_extra.reshape(16, 128)
    key_extra = np.zeros((2, 2, 2, 16, 8, 128), np.float32)
    for a in range(2):
        for b in range(2):
            for p in range(2):
                for row in range(16):
                    for s in range(8):
                        col = 2 * s + p
                        tile_row = (4 * a - 6 + row) // 8 + 1
                        tile_col = (4 * b - 6 + col) // 8 + 1
                        region = tile_row * 3 + tile_col
                        lane = key_extra[a, b, p, row, s]
                        if region != 4:
                            lane[region - (region > 4)] = 1
                        for i in range(4):
                            lane[8 + i] = 0 if i <= row <= i + 2 * RADIUS else AWAY
                            lane[12 + i] = 0 if i <= col <= i + 2 * RADIUS else AWAY
    key_extra = key_extra.reshape(1024, 128)
    stack = lambda x: np.concatenate([x[:, :128], x[:, 128:]], axis=0)
    moving = np.concatenate([stack(double), spread, order, query_extra, key_extra], axis=0).astype(jnp.bfloat16)
    fixed = stack(back).astype(jnp.bfloat16)
    return moving, fixed


def split(x):
    high = x.astype(BF)
    low = (x - high.astype(F32)).astype(BF)
    return high, low


def dot(a, b):
    return jnp.dot(a, b, preferred_element_type=F32)


def dot_t(a, b):
    return lax.dot_general(a, b, (((1,), (1,)), ((), ())), preferred_element_type=F32)


LAG1, LAG2, LAG3 = 2, 4, 6
OUT_AT = 3


def attend_kernel(
    owner_ref, slot_ref, z_ref, q_ref, bias_ref, out_mix_ref, fixed_ref, out_ref, u_ref, placed_ref, made_ref, sems, piece_sems,
):
    me = lax.axis_index("tile")
    low_lane = lax.broadcasted_iota(jnp.int32, (16, 128), 1) < LAT

    sub = lax.broadcasted_iota(jnp.int32, (16, 128), 0) % 8
    ones = jnp.ones((256, 128), BF)

    rows = GROUP * 64
    last = TILES // GROUP

    def place():
        placed_ref[...] = dot(jnp.concatenate([fixed_ref[0:256, :], fixed_ref[256:512, :]], axis=1), u_ref[...]).astype(BF)

    def copy_out(g):
        slot = g % 2
        return pltpu.make_async_copy(
            made_ref.at[slot], out_ref.at[pl.ds(g * rows, rows)], sems.at[slot]
        )

    def body(step, carry):
        @pl.when(step >= 3)
        def _():
            copy_out(step - 3).wait()

        if step:
            place()
        slot = (step + 1) % 2

        def project(n):
            made_ref[slot, :, n * 512 : n * 512 + 512] = dot(
                placed_ref[...], out_mix_ref[:, n * 512 : n * 512 + 512]
            ).astype(BF)

        def region(t):
            tile = step * GROUP + t
            places = []
            for n in range(8):
                owner = owner_ref[n, tile]
                place = HALO + (owner - me) * TILES + slot_ref[n, tile]
                places.append(jnp.where(owner >= 0, place, HALO + tile))
            places = places[:4] + [HALO + tile] + places[4:]
            return tile, [p * 128 for p in places]

        def window(bases, b):
            first, last = ((3, 7), (1, 5))[b]
            sides = []
            for p in range(2):
                strips = []
                for tile_row, pairs in ((0, (1, 2, 3)), (1, (0, 1, 2, 3)), (2, (0, 1, 2))):
                    for pair in pairs:
                        left, mid, right = (
                            z_ref[p, pl.ds(pl.multiple_of(bases[tile_row * 3 + k] + b * 64 + pair * 16, 16), 16), :]
                            for k in range(3)
                        )
                        strips.append(jnp.where(sub < first, left, jnp.where(sub < last, mid, right)))
                sides.append(strips)
            return sides

        work = {}

        def start(i):
            t, b, a = i // 4, i // 2 % 2, i % 2
            quad = 2 * a + b
            if i % 4 == 0:
                work["region"] = region(t)
            tile, bases = work["region"]
            if a == 0:
                work["window"] = window(bases, b)
            even, odd = work["window"]
            cut = slice(2 * a, 2 * a + 8)
            held = jnp.concatenate(even[cut] + odd[cut], axis=0)
            block = q_ref[pl.ds(tile * 64 + quad * 16, 16), :]
            query = jnp.concatenate([block[:, h * 128 : h * 128 + 128] for h in range(HEADS)], axis=0)
            bias = bias_ref[pl.ds(tile * 16, 16), quad * 256 : quad * 256 + 256]
            return held, dot_t(query, held) + jnp.concatenate([bias] * HEADS, axis=0)

        def soften(held, scores):
            raised = jnp.exp2(scores - jnp.max(scores, axis=1, keepdims=True)).astype(BF)
            return held, raised

        def gather(held, raised):
            return dot(raised, jnp.concatenate([held, ones], axis=1))

        def finish(i, summed):
            t, b, a = i // 4, i // 2 % 2, i % 2
            quad = 2 * a + b
            part = summed[:, :128] / summed[:, 128:]
            joined = [
                jnp.where(low_lane, part[32 * k : 32 * k + 16], part[32 * k + 16 : 32 * k + 32])
                for k in range(HEADS // 2)
            ]
            u_ref[pl.ds(t * 64 + quad * 16, 16), :] = jnp.concatenate(joined, axis=1).astype(BF)

        count = GROUP * 4
        scored, softened, gathered = {}, {}, {}
        for i in range(count + LAG3):
            if i < count:
                scored[i] = start(i)
            if i % 4 == OUT_AT and i < count and step:
                project(i // 4)
            j = i - LAG1
            if 0 <= j < count:
                softened[j] = soften(*scored.pop(j))
            j = i - LAG2
            if 0 <= j < count:
                gathered[j] = gather(*softened.pop(j))
            j = i - LAG3
            if 0 <= j < count:
                finish(j, gathered.pop(j))

        @pl.when(step >= 1)
        def _():
            copy_out(step - 1).start()

        return carry

    u_ref[...] = jnp.zeros(u_ref.shape, BF)
    for step in range(last):
        body(step, 0)
    copy_out(last - 3).wait()
    place()
    pieces = []
    for k in range(4):
        cut = slice(k * 512, k * 512 + 512)
        made_ref[(last - 1) % 2, :, cut] = dot(placed_ref[...], out_mix_ref[:, cut]).astype(BF)
        piece = pltpu.make_async_copy(
            made_ref.at[(last - 1) % 2, :, pl.ds(k * 512, 512)],
            out_ref.at[pl.ds((last - 1) * rows, rows), pl.ds(k * 512, 512)], piece_sems.at[k],
        )
        piece.start()
        pieces.append(piece)
    copy_out(last - 2).wait()
    for piece in pieces:
        piece.wait()


def attend(owner, slot, z, q, bias, out_mix, fixed):
    smem = pl.BlockSpec(memory_space=pltpu.SMEM)
    vmem = pl.BlockSpec(memory_space=pltpu.VMEM)
    rows = GROUP * 64
    return pl.pallas_call(
        attend_kernel,
        out_shape=jax.ShapeDtypeStruct((TILES * 64, D), BF),
        in_specs=[smem, smem] + [vmem] * 5,
        out_specs=pl.BlockSpec(memory_space=pl.ANY),
        scratch_shapes=[
            pltpu.VMEM((rows, HEADS * LAT), BF),
            pltpu.VMEM((rows, HEADS * LAT), BF),
            pltpu.VMEM((2, rows, D), BF),
            pltpu.SemaphoreType.DMA((2,)),
            pltpu.SemaphoreType.DMA((4,)),
        ],
        compiler_params=pltpu.CompilerParams(vmem_limit_bytes=24 * 2**20),
        cost_estimate=pl.CostEstimate(flops=8 * 10**9, bytes_accessed=10**7, transcendentals=3 * 10**6),
        name="attend",
    )(owner.T, slot.T, z, q, bias, out_mix, fixed)


CHUNK = 512
MESH = pl.DeviceIdType.MESH


def route_kernel(
    owner_in, latents_ref, embed_in, gain_in, wq_ref, wk_ref, wv_ref, wo_ref,
    moving_in, around_in,
    z_ref, q_ref, bias_ref, out_mix_ref,
    latents, wq, wk, wv, wo, owner_ref, embed_ref, gain_ref, moving, around, mix_ref, stage, outbox, inbox, ext, sems, local_sems,
    send_sem, recv_sem, halo_send, halo_recv,
):
    devices = lax.axis_size("tile")
    me = lax.axis_index("tile")
    edge = HALO * 32

    def load(index, source, target):
        copy = pltpu.make_async_copy(source, target, local_sems.at[index])
        copy.start()
        return copy

    owners = load(0, owner_in, owner_ref)
    loading = load(1, latents_ref, latents)

    barrier = pltpu.get_barrier_semaphore()

    def greet(k, carry):
        pl.semaphore_signal(barrier, inc=1, device_id={"tile": lax.rem(me + k, devices)}, device_id_type=MESH)
        return carry

    lax.fori_loop(1, devices, greet, 0)

    parameters = [load(2, embed_in, embed_ref), load(3, gain_in, gain_ref), load(4, moving_in, moving), load(5, around_in, around)]
    copies = []
    for w, (source, target) in enumerate(((wq_ref, wq), (wk_ref, wk), (wv_ref, wv), (wo_ref, wo))):
        row_count = source.shape[0] // 4
        for c in range(4):
            cut = pl.ds(c * row_count, row_count)
            copy = pltpu.make_async_copy(source.at[cut], target.at[cut], sems.at[w, c])
            copy.start()
            copies.append(copy)

    owners.wait()
    slots = owner_ref.shape[0]
    live = lax.fori_loop(0, slots, lambda j, n: n + jnp.where(owner_ref[j] >= 0, 1, 0), 0)
    dest = lax.broadcasted_iota(jnp.int32, (devices, slots), 0)
    slot = lax.broadcasted_iota(jnp.int32, (devices, slots), 1)
    first = owner_ref[0]
    chosen = jnp.where(((dest - first) % devices == slot) & (slot < live), 1.0, 0.0).astype(BF)
    row = lax.broadcasted_iota(jnp.int32, (devices, 128), 0)
    dead = jnp.where((row - first) % devices < live, 0.0, 512.0)
    loading.wait()
    for n in range(0, TILE_VALUES, 512):
        made = dot(chosen, latents[:, n : n + 512])
        for k in range(4):
            stage[pl.ds(n // 128 + k, devices, stride=32), :] = made[:, k * 128 : k * 128 + 128] + dead

    def pack(d, carry):
        outbox[d] = stage[pl.ds(pl.multiple_of(d * 32, 32), 32), :].astype(BF)
        return carry

    lax.fori_loop(0, devices, pack, 0, unroll=8)
    inbox[me] = outbox[me]
    pl.semaphore_wait(barrier, devices - 1)

    def send(k, carry):
        target = lax.rem(me + k, devices)
        pltpu.make_async_remote_copy(
            src_ref=outbox.at[target], dst_ref=inbox.at[me], send_sem=send_sem, recv_sem=recv_sem,
            device_id={"tile": target}, device_id_type=MESH,
        ).start()
        return carry

    lax.fori_loop(1, devices, send, 0)

    for copy in parameters:
        copy.wait()
    embed = embed_ref[...]
    scaled = embed.astype(F32) * gain_ref[...]
    stacked = jnp.concatenate(split(scaled), axis=0)
    twice = jnp.concatenate([embed, embed], axis=0)
    same = lax.broadcasted_iota(jnp.int32, (128, 128), 0) // LAT == lax.broadcasted_iota(jnp.int32, (128, 128), 1) // LAT
    gram = jnp.concatenate(split(jnp.where(same, dot_t(twice, twice) * (1.0 / D), 0.0)), axis=1)
    block = jnp.where(same, 1.0, 0.0).astype(BF)
    block = jnp.concatenate([block, block], axis=0)

    def folded(w, held):
        total = jnp.zeros((2 * LAT, HEADS * HEAD), F32)
        for c in range(4):
            copies[w * 4 + c].wait()
            total += dot(stacked[:, c * CHUNK : (c + 1) * CHUNK], held[pl.ds(c * CHUNK, CHUNK), :])
        return split(total[:LAT] + total[LAT:])

    query_high, query_low = folded(0, wq)
    key_high, key_low = folded(1, wk)
    for h in range(HEADS):
        cut = slice(h * HEAD, (h + 1) * HEAD)
        left = jnp.concatenate([query_high[:, cut], query_low[:, cut], query_high[:, cut]], axis=1)
        right = jnp.concatenate([key_high[:, cut], key_high[:, cut], key_low[:, cut]], axis=1)
        high, low = split(dot_t(left, jnp.concatenate([right, right], axis=0)) * SCALE)
        mix_ref[:, cut] = jnp.concatenate([high, high, low, low], axis=0)
    everyone = pltpu.make_async_remote_copy(
        src_ref=outbox.at[pl.ds(0, devices - 1)], dst_ref=inbox.at[pl.ds(0, devices - 1)],
        send_sem=send_sem, recv_sem=recv_sem, device_id={"tile": lax.rem(me + 1, devices)}, device_id_type=MESH,
    )
    everyone.wait_recv()

    lane = lax.broadcasted_iota(jnp.int32, (8, 128), 1)

    def rank(source, carry):
        seen, places = carry
        lives = inbox[source, 0:16, :].astype(F32)[:8] < 100.0
        seen = seen + jnp.where(lives, 1, 0)
        return seen, places + jnp.where(seen <= lane, 1, 0)

    zero = jnp.zeros((8, 128), jnp.int32)
    _, places = lax.fori_loop(0, devices, rank, (zero, zero), unroll=8)
    for p in range(TILES):
        ext[pl.ds(edge + p * 32, 32), :] = inbox[jnp.minimum(places[0, p], devices - 1)]
    mine = pl.ds(edge, TILES * 32)
    held = ext[mine, :]
    tall = dot(held, gram)
    wide = held.astype(F32)
    mean = dot(jnp.concatenate(split((tall[:, :128] + tall[:, 128:]) * wide), axis=1), block)
    ext[mine, :] = (wide * lax.rsqrt(jnp.maximum(mean, 0.0) + EPSILON)).astype(BF)

    last = devices - 1

    def halo(side):
        start, end, partner = ((TILES * 32, 0, me + 1), (edge, edge + TILES * 32, me - 1))[side]
        return pltpu.make_async_remote_copy(
            src_ref=ext.at[pl.ds(start, edge)], dst_ref=ext.at[pl.ds(end, edge)],
            send_sem=halo_send.at[side], recv_sem=halo_recv.at[side],
            device_id={"tile": lax.rem(partner + devices, devices)}, device_id_type=MESH,
        )

    @pl.when(me < last)
    def _():
        halo(0).start()

    @pl.when(me > 0)
    def _():
        halo(1).start()

    @pl.when(me == 0)
    def _():
        ext[pl.ds(0, edge), :] = jnp.zeros((edge, 128), BF)

    @pl.when(me == last)
    def _():
        ext[pl.ds(edge + TILES * 32, edge), :] = jnp.zeros((edge, 128), BF)

    rows = GROUP * 32
    order = moving[pl.ds(768, 256), :]
    double = jnp.concatenate([moving[0:128, :], moving[128:256, :]], axis=1)
    spread = moving[pl.ds(256, 512), :]
    parity = (lax.broadcasted_iota(jnp.int32, (GROUP * 64, 128), 0) // 8) % 2
    half = lax.broadcasted_iota(jnp.int32, (GROUP * 64, 128), 1) // LAT
    keep = (parity == half).astype(F32)
    for g in range(TILES // GROUP):
        picked = (dot(order, ext[pl.ds(edge + g * rows, rows), :]) * keep).astype(BF)
        both = jnp.concatenate([picked, picked], axis=1)
        q_ref[pl.ds(g * GROUP * 64, GROUP * 64), :] = dot(both, mix_ref[...]).astype(BF)

    def spread_out(first):
        pair = dot(ext[pl.ds(first * 32, rows), :], double).astype(BF)
        made = dot(spread, pair).astype(BF)
        for p in range(2):
            z_ref[p, pl.ds(first * 128, GROUP * 128), :] = made[:, p * 128 : p * 128 + 128]

    for g in range(TILES // GROUP):
        spread_out(HALO + g * GROUP)
    value = jnp.concatenate(folded(2, wv), axis=0)

    for h in range(HEADS):
        cut = slice(h * HEAD, (h + 1) * HEAD)
        if h % 2 == 0:
            copies[12 + h // 2].wait()
        for n in range(0, D, 512):
            made = dot(value[:, cut], wo[cut, n : n + 512])
            out_mix_ref[pl.ds(h * LAT, LAT), n : n + 512] = (made[:LAT] + made[LAT:]).astype(BF)

    extra_lane = lax.broadcasted_iota(jnp.int32, (16, 128), 1)
    sides = []
    for t in range(TILES):
        side = moving[pl.ds(1024, 16), :].astype(F32)
        for n in range(8):
            side = jnp.where(extra_lane == n, jnp.where(around[n, t] >= 0, 0.0, AWAY).astype(F32), side)
        sides.append(side.astype(BF))
    bias_ref[...] = dot_t(jnp.concatenate(sides, axis=0), moving[pl.ds(1040, 1024), :])
    everyone.wait_send()

    @pl.when(me < last)
    def _():
        halo(0).wait_send()
        halo(1).wait_recv()

    @pl.when(me > 0)
    def _():
        halo(1).wait_send()
        halo(0).wait_recv()

    for start in (0, HALO + TILES):
        for first in (0, 4, 8, HALO - GROUP):
            spread_out(start + first)


def route(tile_owner, tile_latents, w_embed, norm_gain, w_query, w_key, w_value, w_out, moving, around):
    devices = lax.axis_size("tile")
    vmem = pl.BlockSpec(memory_space=pltpu.VMEM)
    hbm = pl.BlockSpec(memory_space=pltpu.HBM)
    dma = pltpu.SemaphoreType.DMA
    return pl.pallas_call(
        route_kernel,
        out_shape=(
            jax.ShapeDtypeStruct((2, EXT * 128, 128), BF),
            jax.ShapeDtypeStruct((TILES * 64, HEADS * HEAD), BF),
            jax.ShapeDtypeStruct((TILES * 16, 1024), F32),
            jax.ShapeDtypeStruct((HEADS * LAT, D), BF),
        ),
        in_specs=[hbm] * 10,
        out_specs=(vmem, vmem, vmem, vmem),
        scratch_shapes=[pltpu.VMEM(tile_latents.shape, BF)]
        + [pltpu.VMEM(w.shape, BF) for w in (w_query, w_key, w_value, w_out)]
        + [
            pltpu.SMEM(tile_owner.shape, jnp.int32),
            pltpu.VMEM(w_embed.shape, BF),
            pltpu.VMEM((1, D), F32),
            pltpu.VMEM(moving.shape, BF),
            pltpu.SMEM(around.shape, jnp.int32),
            pltpu.VMEM((4 * LAT, HEADS * HEAD), BF),
            pltpu.VMEM((devices * 32, 128), F32),
            pltpu.VMEM((devices, 32, 128), BF),
            pltpu.VMEM((devices, 32, 128), BF),
            pltpu.VMEM((EXT * 32, 128), BF),
            dma((4, 4)), dma((6,)), dma, dma, dma((2,)), dma((2,)),
        ],
        compiler_params=pltpu.CompilerParams(
            vmem_limit_bytes=40 * 2**20, collective_id=0, has_side_effects=True
        ),
        cost_estimate=pl.CostEstimate(flops=3 * 10**9, bytes_accessed=2 * 10**7, transcendentals=0),
        name="route",
    )(
        *[
            pltpu.with_memory_space_constraint(x, pltpu.HBM)
            for x in (
                tile_owner, tile_latents, w_embed, norm_gain.reshape(1, D), w_query, w_key, w_value, w_out, moving,
                around,
            )
        ],
    )


def local(
    tile_latents, tile_owner, tile_position, neighbour_owner, neighbour_slot,
    w_embed, norm_gain, w_query, w_key, w_value, w_out,
):
    moving, fixed = (jnp.asarray(c) for c in place_constants())
    z, q, bias, out_mix = route(
        tile_owner, tile_latents, w_embed, norm_gain, w_query, w_key, w_value, w_out, moving, neighbour_owner.T
    )
    return attend(neighbour_owner, neighbour_slot, z, q, bias, out_mix, fixed)


def solution(mesh):
    both = P(("dp", "tile"), None)
    flat = P(("dp", "tile"))
    return jax.shard_map(
        local,
        mesh=mesh,
        in_specs=(both, flat, flat, both, both, P(), P(), P(), P(), P(), P()),
        out_specs=both,
        check_vma=False,
    )
```

```python
import math

import jax
import jax.numpy as jnp
import numpy as np
from jax import lax
from jax.experimental import pallas as pl
from jax.experimental.pallas import tpu as pltpu
from jax.sharding import PartitionSpec as P

D = 2048
HEADS = 8
HEAD = 128
LAT = 64
SIDE = 8
RADIUS = 6
HALO = 14
TILES = 24
TILE_VALUES = 4096
EXT = TILES + 2 * HALO
EPSILON = 1e-06
AWAY = -1e38
GROUP = 4
SCALE = 0.5 * HEAD ** -0.5 * math.log2(math.e)

BF = jnp.bfloat16
F32 = jnp.float32


def place_constants():
    double = np.zeros((2, LAT, 2, 2, LAT), np.float32)
    for p in range(2):
        for k in range(LAT):
            double[p, k, p, :, k] = 1
    double = double.reshape(128, 256)
    spread = np.zeros((GROUP, 2, 8, 8, GROUP, 8, 4), np.float32)
    for t in range(GROUP):
        for form in range(2):
            for r in range(8):
                for s in range(8):
                    spread[t, form, r, s, t, r, (s + 1 + 2 * form) % 4] = 1
    spread = spread.reshape(GROUP * 128, GROUP * 32)
    order = np.zeros((GROUP, 2, 2, 2, 4, 2, GROUP, 8, 4), np.float32)
    back = np.zeros((GROUP, 8, 8, GROUP, 2, 2, 2, 4, 2), np.float32)
    for t in range(GROUP):
        for a in range(2):
            for b in range(2):
                for p in range(2):
                    for r in range(4):
                        for c in range(2):
                            order[t, a, b, p, r, c, t, 4 * a + r, 2 * b + c] = 1
                            back[t, 4 * a + r, 4 * b + 2 * c + p, t, a, b, p, r, c] = 1
    order = order.reshape(GROUP * 64, GROUP * 32)
    back = back.reshape(GROUP * 64, GROUP * 64)
    query_extra = np.zeros((2, 4, 2, 128), np.float32)
    for p in range(2):
        for r in range(4):
            for c in range(2):
                query_extra[p, r, c, 8 + r] = 1
                query_extra[p, r, c, 12 + 2 * c + p] = 1
    query_extra = query_extra.reshape(16, 128)
    key_extra = np.zeros((2, 2, 2, 16, 8, 128), np.float32)
    for a in range(2):
        for b in range(2):
            for p in range(2):
                for row in range(16):
                    for s in range(8):
                        col = 2 * s + p
                        tile_row = (4 * a - 6 + row) // 8 + 1
                        tile_col = (4 * b - 6 + col) // 8 + 1
                        region = tile_row * 3 + tile_col
                        lane = key_extra[a, b, p, row, s]
                        if region != 4:
                            lane[region - (region > 4)] = 1
                        for i in range(4):
                            lane[8 + i] = 0 if i <= row <= i + 2 * RADIUS else AWAY
                            lane[12 + i] = 0 if i <= col <= i + 2 * RADIUS else AWAY
    key_extra = key_extra.reshape(1024, 128)
    stack = lambda x: np.concatenate([x[:, :128], x[:, 128:]], axis=0)
    moving = np.concatenate([stack(double), spread, order, query_extra, key_extra], axis=0).astype(jnp.bfloat16)
    fixed = stack(back).astype(jnp.bfloat16)
    return moving, fixed


def split(x):
    high = x.astype(BF)
    low = (x - high.astype(F32)).astype(BF)
    return high, low


def dot(a, b):
    return jnp.dot(a, b, preferred_element_type=F32)


def dot_t(a, b):
    return lax.dot_general(a, b, (((1,), (1,)), ((), ())), preferred_element_type=F32)


LAG1, LAG2, LAG3 = 2, 4, 6
OUT_AT = 3


def attend_kernel(
    owner_ref, slot_ref, z_ref, q_ref, bias_ref, out_mix_ref, fixed_ref, out_ref, u_ref, placed_ref, made_ref, sems, piece_sems,
):
    me = lax.axis_index("tile")
    low_lane = lax.broadcasted_iota(jnp.int32, (16, 128), 1) < LAT

    sub = lax.broadcasted_iota(jnp.int32, (16, 128), 0) % 8
    ones = jnp.ones((256, 128), BF)

    rows = GROUP * 64
    last = TILES // GROUP

    def place():
        placed_ref[...] = dot(jnp.concatenate([fixed_ref[0:256, :], fixed_ref[256:512, :]], axis=1), u_ref[...]).astype(BF)

    def copy_out(g):
        slot = g % 2
        return pltpu.make_async_copy(
            made_ref.at[slot], out_ref.at[pl.ds(g * rows, rows)], sems.at[slot]
        )

    def body(step, carry):
        @pl.when(step >= 3)
        def _():
            copy_out(step - 3).wait()

        if step:
            place()
        slot = (step + 1) % 2

        def project(n):
            made_ref[slot, :, n * 512 : n * 512 + 512] = dot(
                placed_ref[...], out_mix_ref[:, n * 512 : n * 512 + 512]
            ).astype(BF)

        def region(t):
            tile = step * GROUP + t
            places = []
            for n in range(8):
                owner = owner_ref[n, tile]
                place = HALO + (owner - me) * TILES + slot_ref[n, tile]
                places.append(jnp.where(owner >= 0, place, HALO + tile))
            places = places[:4] + [HALO + tile] + places[4:]
            return tile, [p * 128 for p in places]

        def window(bases, b):
            first, last = ((3, 7), (1, 5))[b]
            sides = []
            for p in range(2):
                strips = []
                for tile_row, pairs in ((0, (1, 2, 3)), (1, (0, 1, 2, 3)), (2, (0, 1, 2))):
                    for pair in pairs:
                        left, mid, right = (
                            z_ref[p, pl.ds(pl.multiple_of(bases[tile_row * 3 + k] + b * 64 + pair * 16, 16), 16), :]
                            for k in range(3)
                        )
                        strips.append(jnp.where(sub < first, left, jnp.where(sub < last, mid, right)))
                sides.append(strips)
            return sides

        work = {}

        def start(i):
            t, b, a = i // 4, i // 2 % 2, i % 2
            quad = 2 * a + b
            if i % 4 == 0:
                work["region"] = region(t)
            tile, bases = work["region"]
            if a == 0:
                work["window"] = window(bases, b)
            even, odd = work["window"]
            cut = slice(2 * a, 2 * a + 8)
            held = jnp.concatenate(even[cut] + odd[cut], axis=0)
            block = q_ref[pl.ds(tile * 64 + quad * 16, 16), :]
            query = jnp.concatenate([block[:, h * 128 : h * 128 + 128] for h in range(HEADS)], axis=0)
            bias = bias_ref[pl.ds(tile * 16, 16), quad * 256 : quad * 256 + 256]
            return held, dot_t(query, held) + jnp.concatenate([bias] * HEADS, axis=0)

        def soften(held, scores):
            raised = jnp.exp2(scores - jnp.max(scores, axis=1, keepdims=True)).astype(BF)
            return held, raised

        def gather(held, raised):
            return dot(raised, jnp.concatenate([held, ones], axis=1))

        def finish(i, summed):
            t, b, a = i // 4, i // 2 % 2, i % 2
            quad = 2 * a + b
            part = summed[:, :128] / summed[:, 128:]
            joined = [
                jnp.where(low_lane, part[32 * k : 32 * k + 16], part[32 * k + 16 : 32 * k + 32])
                for k in range(HEADS // 2)
            ]
            u_ref[pl.ds(t * 64 + quad * 16, 16), :] = jnp.concatenate(joined, axis=1).astype(BF)

        count = GROUP * 4
        scored, softened, gathered = {}, {}, {}
        for i in range(count + LAG3):
            if i < count:
                scored[i] = start(i)
            if i % 4 == OUT_AT and i < count and step:
                project(i // 4)
            j = i - LAG1
            if 0 <= j < count:
                softened[j] = soften(*scored.pop(j))
            j = i - LAG2
            if 0 <= j < count:
                gathered[j] = gather(*softened.pop(j))
            j = i - LAG3
            if 0 <= j < count:
                finish(j, gathered.pop(j))

        @pl.when(step >= 1)
        def _():
            copy_out(step - 1).start()

        return carry

    u_ref[...] = jnp.zeros(u_ref.shape, BF)
    for step in range(last):
        body(step, 0)
    copy_out(last - 3).wait()
    place()
    pieces = []
    for k in range(4):
        cut = slice(k * 512, k * 512 + 512)
        made_ref[(last - 1) % 2, :, cut] = dot(placed_ref[...], out_mix_ref[:, cut]).astype(BF)
        piece = pltpu.make_async_copy(
            made_ref.at[(last - 1) % 2, :, pl.ds(k * 512, 512)],
            out_ref.at[pl.ds((last - 1) * rows, rows), pl.ds(k * 512, 512)], piece_sems.at[k],
        )
        piece.start()
        pieces.append(piece)
    copy_out(last - 2).wait()
    for piece in pieces:
        piece.wait()


def attend(owner, slot, z, q, bias, out_mix, fixed):
    smem = pl.BlockSpec(memory_space=pltpu.SMEM)
    vmem = pl.BlockSpec(memory_space=pltpu.VMEM)
    rows = GROUP * 64
    return pl.pallas_call(
        attend_kernel,
        out_shape=jax.ShapeDtypeStruct((TILES * 64, D), BF),
        in_specs=[smem, smem] + [vmem] * 5,
        out_specs=pl.BlockSpec(memory_space=pl.ANY),
        scratch_shapes=[
            pltpu.VMEM((rows, HEADS * LAT), BF),
            pltpu.VMEM((rows, HEADS * LAT), BF),
            pltpu.VMEM((2, rows, D), BF),
            pltpu.SemaphoreType.DMA((2,)),
            pltpu.SemaphoreType.DMA((4,)),
        ],
        compiler_params=pltpu.CompilerParams(vmem_limit_bytes=24 * 2**20),
        cost_estimate=pl.CostEstimate(flops=8 * 10**9, bytes_accessed=10**7, transcendentals=3 * 10**6),
        name="attend",
    )(owner.T, slot.T, z, q, bias, out_mix, fixed)


CHUNK = 512
MESH = pl.DeviceIdType.MESH


def route_kernel(
    owner_in, latents_ref, embed_in, gain_in, wq_ref, wk_ref, wv_ref, wo_ref,
    moving_in, around_in,
    z_ref, q_ref, bias_ref, out_mix_ref,
    latents, wq, wk, wv, wo, owner_ref, embed_ref, gain_ref, moving, around, mix_ref, stage, outbox, inbox, ext, sems, local_sems,
    send_sem, recv_sem, halo_send, halo_recv,
):
    devices = lax.axis_size("tile")
    me = lax.axis_index("tile")
    edge = HALO * 32

    def load(index, source, target):
        copy = pltpu.make_async_copy(source, target, local_sems.at[index])
        copy.start()
        return copy

    owners = load(0, owner_in, owner_ref)
    loading = load(1, latents_ref, latents)

    barrier = pltpu.get_barrier_semaphore()

    def greet(k, carry):
        pl.semaphore_signal(barrier, inc=1, device_id={"tile": lax.rem(me + k, devices)}, device_id_type=MESH)
        return carry

    lax.fori_loop(1, devices, greet, 0, unroll=7)

    parameters = [load(2, embed_in, embed_ref), load(3, gain_in, gain_ref), load(4, moving_in, moving), load(5, around_in, around)]
    copies = []
    for w, (source, target) in enumerate(((wq_ref, wq), (wk_ref, wk), (wv_ref, wv), (wo_ref, wo))):
        row_count = source.shape[0] // 4
        for c in range(4):
            cut = pl.ds(c * row_count, row_count)
            copy = pltpu.make_async_copy(source.at[cut], target.at[cut], sems.at[w, c])
            copy.start()
            copies.append(copy)

    owners.wait()
    slots = owner_ref.shape[0]
    live = lax.fori_loop(0, slots, lambda j, n: n + jnp.where(owner_ref[j] >= 0, 1, 0), 0)
    dest = lax.broadcasted_iota(jnp.int32, (devices, slots), 0)
    slot = lax.broadcasted_iota(jnp.int32, (devices, slots), 1)
    first = owner_ref[0]
    chosen = jnp.where(((dest - first) % devices == slot) & (slot < live), 1.0, 0.0).astype(BF)
    row = lax.broadcasted_iota(jnp.int32, (devices, 128), 0)
    dead = jnp.where((row - first) % devices < live, 0.0, 512.0)
    loading.wait()
    for n in range(0, TILE_VALUES, 512):
        made = dot(chosen, latents[:, n : n + 512])
        for k in range(4):
            stage[pl.ds(n // 128 + k, devices, stride=32), :] = made[:, k * 128 : k * 128 + 128] + dead

    def pack(d, carry):
        outbox[d] = stage[pl.ds(pl.multiple_of(d * 32, 32), 32), :].astype(BF)
        return carry

    lax.fori_loop(0, devices, pack, 0, unroll=8)
    inbox[me] = outbox[me]
    pl.semaphore_wait(barrier, devices - 1)

    def send(k, carry):
        target = lax.rem(me + k, devices)
        pltpu.make_async_remote_copy(
            src_ref=outbox.at[target], dst_ref=inbox.at[me], send_sem=send_sem, recv_sem=recv_sem,
            device_id={"tile": target}, device_id_type=MESH,
        ).start()
        return carry

    lax.fori_loop(1, devices, send, 0, unroll=7)

    for copy in parameters:
        copy.wait()
    embed = embed_ref[...]
    scaled = embed.astype(F32) * gain_ref[...]
    stacked = jnp.concatenate(split(scaled), axis=0)
    twice = jnp.concatenate([embed, embed], axis=0)
    same = lax.broadcasted_iota(jnp.int32, (128, 128), 0) // LAT == lax.broadcasted_iota(jnp.int32, (128, 128), 1) // LAT
    gram = jnp.concatenate(split(jnp.where(same, dot_t(twice, twice) * (1.0 / D), 0.0)), axis=1)
    block = jnp.where(same, 1.0, 0.0).astype(BF)
    block = jnp.concatenate([block, block], axis=0)

    def folded(w, held):
        total = jnp.zeros((2 * LAT, HEADS * HEAD), F32)
        for c in range(4):
            copies[w * 4 + c].wait()
            total += dot(stacked[:, c * CHUNK : (c + 1) * CHUNK], held[pl.ds(c * CHUNK, CHUNK), :])
        return split(total[:LAT] + total[LAT:])

    query_high, query_low = folded(0, wq)
    key_high, key_low = folded(1, wk)
    for h in range(HEADS):
        cut = slice(h * HEAD, (h + 1) * HEAD)
        left = jnp.concatenate([query_high[:, cut], query_low[:, cut], query_high[:, cut]], axis=1)
        right = jnp.concatenate([key_high[:, cut], key_high[:, cut], key_low[:, cut]], axis=1)
        high, low = split(dot_t(left, jnp.concatenate([right, right], axis=0)) * SCALE)
        mix_ref[:, cut] = jnp.concatenate([high, high, low, low], axis=0)
    everyone = pltpu.make_async_remote_copy(
        src_ref=outbox.at[pl.ds(0, devices - 1)], dst_ref=inbox.at[pl.ds(0, devices - 1)],
        send_sem=send_sem, recv_sem=recv_sem, device_id={"tile": lax.rem(me + 1, devices)}, device_id_type=MESH,
    )
    everyone.wait_recv()

    lane = lax.broadcasted_iota(jnp.int32, (8, 128), 1)

    def rank(source, carry):
        seen, places = carry
        lives = inbox[source, 0:16, :].astype(F32)[:8] < 100.0
        seen = seen + jnp.where(lives, 1, 0)
        return seen, places + jnp.where(seen <= lane, 1, 0)

    zero = jnp.zeros((8, 128), jnp.int32)
    _, places = lax.fori_loop(0, devices, rank, (zero, zero), unroll=16)
    for p in range(TILES):
        ext[pl.ds(edge + p * 32, 32), :] = inbox[jnp.minimum(places[0, p], devices - 1)]
    mine = pl.ds(edge, TILES * 32)
    held = ext[mine, :]
    tall = dot(held, gram)
    wide = held.astype(F32)
    mean = dot(jnp.concatenate(split((tall[:, :128] + tall[:, 128:]) * wide), axis=1), block)
    ext[mine, :] = (wide * lax.rsqrt(jnp.maximum(mean, 0.0) + EPSILON)).astype(BF)

    last = devices - 1

    def halo(side):
        start, end, partner = ((TILES * 32, 0, me + 1), (edge, edge + TILES * 32, me - 1))[side]
        return pltpu.make_async_remote_copy(
            src_ref=ext.at[pl.ds(start, edge)], dst_ref=ext.at[pl.ds(end, edge)],
            send_sem=halo_send.at[side], recv_sem=halo_recv.at[side],
            device_id={"tile": lax.rem(partner + devices, devices)}, device_id_type=MESH,
        )

    @pl.when(me < last)
    def _():
        halo(0).start()

    @pl.when(me > 0)
    def _():
        halo(1).start()

    @pl.when(me == 0)
    def _():
        ext[pl.ds(0, edge), :] = jnp.zeros((edge, 128), BF)

    @pl.when(me == last)
    def _():
        ext[pl.ds(edge + TILES * 32, edge), :] = jnp.zeros((edge, 128), BF)

    rows = GROUP * 32
    order = moving[pl.ds(768, 256), :]
    double = jnp.concatenate([moving[0:128, :], moving[128:256, :]], axis=1)
    spread = moving[pl.ds(256, 512), :]
    parity = (lax.broadcasted_iota(jnp.int32, (GROUP * 64, 128), 0) // 8) % 2
    half = lax.broadcasted_iota(jnp.int32, (GROUP * 64, 128), 1) // LAT
    keep = (parity == half).astype(F32)
    for g in range(TILES // GROUP):
        picked = (dot(order, ext[pl.ds(edge + g * rows, rows), :]) * keep).astype(BF)
        both = jnp.concatenate([picked, picked], axis=1)
        q_ref[pl.ds(g * GROUP * 64, GROUP * 64), :] = dot(both, mix_ref[...]).astype(BF)

    def spread_out(first):
        pair = dot(ext[pl.ds(first * 32, rows), :], double).astype(BF)
        made = dot(spread, pair).astype(BF)
        for p in range(2):
            z_ref[p, pl.ds(first * 128, GROUP * 128), :] = made[:, p * 128 : p * 128 + 128]

    for g in range(TILES // GROUP):
        spread_out(HALO + g * GROUP)
    value = jnp.concatenate(folded(2, wv), axis=0)

    for h in range(HEADS):
        cut = slice(h * HEAD, (h + 1) * HEAD)
        if h % 2 == 0:
            copies[12 + h // 2].wait()
        for n in range(0, D, 512):
            made = dot(value[:, cut], wo[cut, n : n + 512])
            out_mix_ref[pl.ds(h * LAT, LAT), n : n + 512] = (made[:LAT] + made[LAT:]).astype(BF)

    extra_lane = lax.broadcasted_iota(jnp.int32, (16, 128), 1)
    sides = []
    for t in range(TILES):
        side = moving[pl.ds(1024, 16), :].astype(F32)
        for n in range(8):
            side = jnp.where(extra_lane == n, jnp.where(around[n, t] >= 0, 0.0, AWAY).astype(F32), side)
        sides.append(side.astype(BF))
    bias_ref[...] = dot_t(jnp.concatenate(sides, axis=0), moving[pl.ds(1040, 1024), :])
    everyone.wait_send()

    @pl.when(me < last)
    def _():
        halo(0).wait_send()
        halo(1).wait_recv()

    @pl.when(me > 0)
    def _():
        halo(1).wait_send()
        halo(0).wait_recv()

    for start in (0, HALO + TILES):
        for first in (0, 4, 8, HALO - GROUP):
            spread_out(start + first)


def route(tile_owner, tile_latents, w_embed, norm_gain, w_query, w_key, w_value, w_out, moving, around):
    devices = lax.axis_size("tile")
    vmem = pl.BlockSpec(memory_space=pltpu.VMEM)
    hbm = pl.BlockSpec(memory_space=pltpu.HBM)
    dma = pltpu.SemaphoreType.DMA
    return pl.pallas_call(
        route_kernel,
        out_shape=(
            jax.ShapeDtypeStruct((2, EXT * 128, 128), BF),
            jax.ShapeDtypeStruct((TILES * 64, HEADS * HEAD), BF),
            jax.ShapeDtypeStruct((TILES * 16, 1024), F32),
            jax.ShapeDtypeStruct((HEADS * LAT, D), BF),
        ),
        in_specs=[hbm] * 10,
        out_specs=(vmem, vmem, vmem, vmem),
        scratch_shapes=[pltpu.VMEM(tile_latents.shape, BF)]
        + [pltpu.VMEM(w.shape, BF) for w in (w_query, w_key, w_value, w_out)]
        + [
            pltpu.SMEM(tile_owner.shape, jnp.int32),
            pltpu.VMEM(w_embed.shape, BF),
            pltpu.VMEM((1, D), F32),
            pltpu.VMEM(moving.shape, BF),
            pltpu.SMEM(around.shape, jnp.int32),
            pltpu.VMEM((4 * LAT, HEADS * HEAD), BF),
            pltpu.VMEM((devices * 32, 128), F32),
            pltpu.VMEM((devices, 32, 128), BF),
            pltpu.VMEM((devices, 32, 128), BF),
            pltpu.VMEM((EXT * 32, 128), BF),
            dma((4, 4)), dma((6,)), dma, dma, dma((2,)), dma((2,)),
        ],
        compiler_params=pltpu.CompilerParams(
            vmem_limit_bytes=40 * 2**20, collective_id=0, has_side_effects=True
        ),
        cost_estimate=pl.CostEstimate(flops=3 * 10**9, bytes_accessed=2 * 10**7, transcendentals=0),
        name="route",
    )(
        *[
            pltpu.with_memory_space_constraint(x, pltpu.HBM)
            for x in (
                tile_owner, tile_latents, w_embed, norm_gain.reshape(1, D), w_query, w_key, w_value, w_out, moving,
                around,
            )
        ],
    )


def local(
    tile_latents, tile_owner, tile_position, neighbour_owner, neighbour_slot,
    w_embed, norm_gain, w_query, w_key, w_value, w_out,
):
    moving, fixed = (jnp.asarray(c) for c in place_constants())
    z, q, bias, out_mix = route(
        tile_owner, tile_latents, w_embed, norm_gain, w_query, w_key, w_value, w_out, moving, neighbour_owner.T
    )
    return attend(neighbour_owner, neighbour_slot, z, q, bias, out_mix, fixed)


def solution(mesh):
    both = P(("dp", "tile"), None)
    flat = P(("dp", "tile"))
    return jax.shard_map(
        local,
        mesh=mesh,
        in_specs=(both, flat, flat, both, both, P(), P(), P(), P(), P(), P()),
        out_specs=both,
        check_vma=False,
    )
```
